128 devices in a mesh: dp: 4 (over x), depth: 32 (over z, y, core).
Axes of the slice: x: 4, y: 4, z: 4, core: 2. Of those that a mesh axis runs over, the one named last changes fastest.
Arguments:
- c_states: float32 [32, 1024, 1024], P('depth', 'dp'), parts along dimension 1, may hold values from -20 to 20
- w_query: bfloat16 [64, 1024, 1024], P('depth'), may hold values from -16 to 16
- w_key: bfloat16 [64, 1024, 1024], P('depth'), may hold values from -8 to 8
- w_value: bfloat16 [64, 1024, 1024], P('depth'), may hold values from -0.1875 to 0.1875
- w_out: bfloat16 [64, 1024, 1024], P('depth'), may hold values from -0.1875 to 0.1875
Outputs:
- states: float32 [64, 1024, 1024], P('depth', 'dp'), parts along dimension 1
- residual_rms: float32 [4], P('dp'), parts along dimension 0
The draws below stay inside these ranges and needn't reach their ends.
There are 4 independent parts, one for each index of `dp`. The reference program is written for one: setup_inputs(seed, part) draws one part's arguments, and reference() takes and returns one part's arrays. A program takes and returns all parts, laid end to end along the dimension named above; an argument that names none is the same for every part. Nothing has to cross between parts.
All inputs are finite; a program needn't handle non-finite values.
Results may differ from the reference program's by a relative error of at most 0.006.
Values sent between devices are 32-bit elements; how exact they have to be, the bound alone decides.
No kernel may reach another device: no remote copies, remote signals or barrier semaphores. Data moves between devices by JAX's collectives and lax.ppermute only.
A program may use at most 384 MiB of HBM per device.

```python
import jax
import jax.numpy as jnp
from jax import lax

D = 1024
HEADS = 8
HEAD_DIM = 128
SEQ = 256
INNER = 1024
LAYERS = 64
C_POINTS = 32


def draw_w_query(key, part):
    key = jax.random.fold_in(key, 1)
    return (jax.random.normal(key, (LAYERS, D, INNER), jnp.float32) * D ** (-0.5)).astype(jnp.bfloat16)


def draw_w_key(key, part):
    key = jax.random.fold_in(key, 2)
    return jnp.clip(jax.random.normal(key, (LAYERS, D, INNER), jnp.float32) * D ** (-0.5), -8.0, 8.0).astype(jnp.bfloat16)


def draw_c_states(key, part):
    key = jax.random.fold_in(key, 3)
    ramp = jnp.arange(C_POINTS, dtype=jnp.float32) / max(C_POINTS - 1, 1)
    values = jnp.clip(jax.random.normal(key, (C_POINTS, SEQ, D), jnp.float32), -6.0, 6.0)
    full = values * (1.0 + 2.0 * ramp)[:, None, None]
    return full


def level_of(key, dims, cuts, low, high):
    def one(axis_at, parts):
        draws = jax.random.uniform(jax.random.fold_in(jax.random.fold_in(key, 6), axis_at), (parts,), jnp.float32, low / len(cuts), high / len(cuts))
        return jnp.repeat(jnp.exp(draws), dims[axis_at] // parts).reshape((-1,) + (1,) * (len(dims) - axis_at - 1))

    loudness = one(*cuts[0])
    for cut in cuts[1:]:
        loudness = loudness * one(*cut)
    return loudness


def scatter_about(stream_key, dims, deviation, limit, shards=(), kind=jnp.bfloat16):
    values = deviation * jax.random.normal(stream_key, dims, jnp.float32)
    if shards:
        values = values * level_of(stream_key, dims, shards, -0.22, 0.18)
    return jnp.clip(values, -limit, limit).astype(kind)


def setup_inputs(seed: int = 0, part: int = 0) -> dict:
    streams_of = jax.random.split(jax.random.key(seed), 6)
    part_keys = jax.random.split(jax.random.fold_in(streams_of[5], part), 6)
    return {
        "c_states": draw_c_states(jax.random.fold_in(jax.random.fold_in(streams_of[5], part), 71), part),
        "w_query": draw_w_query(jax.random.fold_in(streams_of[5], 71), part),
        "w_key": draw_w_key(jax.random.fold_in(streams_of[5], 71), part),
        "w_value": scatter_about(streams_of[3], (LAYERS, D, INNER), D ** -0.5, 0.1875, ((0, 32),)),
        "w_out": scatter_about(streams_of[4], (LAYERS, INNER, D), INNER ** -0.5, 0.1875, ((0, 32),)),
    }


def normalize_rows(state):
    row_mean = lax.optimization_barrier(jnp.mean(state, axis=-1, keepdims=True))
    centred = state - row_mean
    row_var = lax.optimization_barrier(jnp.mean(centred * centred, axis=-1, keepdims=True))
    return centred * lax.rsqrt(row_var + 1e-05)

def apply_layer(state, w_query, w_key, w_value, w_out):
    tokens = state.shape[0]
    normed = normalize_rows(state).astype(jnp.bfloat16)
    query_rows = jnp.dot(normed, w_query, preferred_element_type=jnp.float32).astype(jnp.bfloat16)
    key_rows = jnp.dot(normed, w_key, preferred_element_type=jnp.float32).astype(jnp.bfloat16)
    value_rows = jnp.dot(normed, w_value, preferred_element_type=jnp.float32).astype(jnp.bfloat16)
    query_heads = query_rows.reshape(tokens, HEADS, HEAD_DIM).astype(jnp.float32)
    key_heads = key_rows.reshape(tokens, HEADS, HEAD_DIM).astype(jnp.float32)
    value_heads = value_rows.reshape(tokens, HEADS, HEAD_DIM).astype(jnp.float32)
    scores = jnp.einsum('qhd,khd->hqk', query_heads, key_heads) * HEAD_DIM ** (-0.5)
    attn_probs = jax.nn.softmax(scores, axis=-1).astype(jnp.bfloat16)
    context = jnp.einsum('hqk,khd->qhd', attn_probs.astype(jnp.float32), value_heads)
    context = context.reshape(tokens, INNER).astype(jnp.bfloat16)
    return state + jnp.dot(context, w_out, preferred_element_type=jnp.float32)

def reference(c_states, w_query, w_key, w_value, w_out):
    points = c_states.shape[0]
    tokens = c_states.shape[1]
    width = c_states.shape[2]
    guesses = c_states
    identity_m = jnp.eye(width, dtype=jnp.float32)
    advanced = []
    coarse_maps = []
    for point in range(points):
        first = 2 * point
        fine_f = apply_layer(guesses[point], w_query[first], w_key[first], w_value[first], w_out[first])
        fine_c = apply_layer(fine_f, w_query[first + 1], w_key[first + 1], w_value[first + 1], w_out[first + 1])
        advanced.append(fine_c)
        product = jnp.dot(w_value[first + 1], w_out[first + 1], preferred_element_type=jnp.float32)
        coarse_maps.append(identity_m + 0.25 * product)
    total_sq = jnp.zeros((), jnp.float32)
    correction = jnp.zeros((tokens, width), jnp.float32)
    out_list = []
    for point in range(points):
        first = 2 * point
        out_list.append(apply_layer(guesses[point] + correction, w_query[first], w_key[first], w_value[first], w_out[first]))
        carried = jnp.dot(correction, coarse_maps[point], precision=lax.Precision.HIGHEST)
        out_list.append(advanced[point] + carried)
        if point + 1 < points:
            residual = advanced[point] - guesses[point + 1]
            total_sq = total_sq + jnp.sum(residual * residual)
            correction = carried + residual
    residual_rms = jnp.sqrt(total_sq / ((points - 1) * tokens * width)).reshape(1)
    return (jnp.stack(out_list), residual_rms)
```

```python
import functools

import jax
import jax.numpy as jnp
from jax import lax
from jax.experimental import pallas as pl
from jax.experimental.pallas import tpu as pltpu
from jax.sharding import PartitionSpec as P

HEADS = 8
HEAD_DIM = 128
INNER = 1024
CHUNKS = 4

BF = jnp.bfloat16
F32 = jnp.float32
IN_VMEM = pl.BlockSpec(memory_space=pltpu.VMEM)
IN_SMEM = pl.BlockSpec(memory_space=pltpu.SMEM)


def normalize_rows(state):
    row_mean = jnp.mean(state, axis=-1, keepdims=True)
    centred = state - row_mean
    row_var = jnp.mean(centred * centred, axis=-1, keepdims=True)
    return centred * lax.rsqrt(row_var + 1e-05)


def apply_layer(state, w_query, w_key, w_value, w_out):
    tokens = state.shape[0]
    normed = normalize_rows(state).astype(jnp.bfloat16)
    query_rows = jnp.dot(normed, w_query, preferred_element_type=jnp.float32).astype(jnp.bfloat16)
    key_rows = jnp.dot(normed, w_key, preferred_element_type=jnp.float32).astype(jnp.bfloat16)
    value_rows = jnp.dot(normed, w_value, preferred_element_type=jnp.float32).astype(jnp.bfloat16)
    query_heads = query_rows.reshape(tokens, HEADS, HEAD_DIM)
    key_heads = key_rows.reshape(tokens, HEADS, HEAD_DIM)
    value_heads = value_rows.reshape(tokens, HEADS, HEAD_DIM)
    scores = jnp.einsum(
        "qhd,khd->hqk", query_heads, key_heads, preferred_element_type=jnp.float32
    ) * HEAD_DIM ** (-0.5)
    attn_probs = jax.nn.softmax(scores, axis=-1).astype(jnp.bfloat16)
    context = jnp.einsum(
        "hqk,khd->qhd", attn_probs, value_heads, preferred_element_type=jnp.float32
    )
    context = context.reshape(tokens, INNER).astype(jnp.bfloat16)
    return state + jnp.dot(context, w_out, preferred_element_type=jnp.float32)


def halves(value):
    high = value.astype(BF)
    return high, (value - high.astype(F32)).astype(BF)


def split_dot(left, right_high, right_low):
    rows = left.shape[0]
    high, low = halves(left)
    both = jnp.dot(jnp.concatenate([high, low], 0), right_high, preferred_element_type=F32)
    return both[:rows] + both[rows:] + jnp.dot(high, right_low, preferred_element_type=F32)


def in_vmem(*arrays):
    return tuple(pltpu.with_memory_space_constraint(a, pltpu.VMEM) for a in arrays)


def call(kernel, outs, n_in, flops, limit=40):
    return pl.pallas_call(
        kernel,
        out_shape=outs,
        in_specs=[IN_SMEM] + [IN_VMEM] * (n_in - 1),
        out_specs=jax.tree.map(lambda _: IN_VMEM, outs),
        compiler_params=pltpu.CompilerParams(vmem_limit_bytes=limit << 20),
        cost_estimate=pl.CostEstimate(flops=flops, bytes_accessed=1 << 20, transcendentals=0),
    )


def parts_kernel(core, own, other, b0_high, b0_low, b1_high, b1_low):
    first = core[0] == 0

    @pl.loop(0, own.shape[0] // 128)
    def _(block):
        rows = pl.ds(pl.multiple_of(block * 128, 128), 128)
        mine, theirs = own[rows, :], other[rows, :]
        b0_high[rows, :], b0_low[rows, :] = halves(jnp.where(first, mine, theirs))
        b1_high[rows, :], b1_low[rows, :] = halves(jnp.where(first, theirs, mine))


def product_kernel(core, own, other, b0_high, b0_low, b1_high, b1_low, c_high, c_low):
    @pl.loop(0, own.shape[0] // 256)
    def _(block):
        rows = pl.ds(pl.multiple_of(block * 256, 256), 256)
        high, low = b0_high[rows, :], b0_low[rows, :]
        both = jnp.dot(jnp.concatenate([high, low], 0), b1_high[...], preferred_element_type=F32)
        total = both[:256] + both[256:] + jnp.dot(high, b1_low[...], preferred_element_type=F32)
        total = total + (own[rows, :] + other[rows, :])
        c_high[rows, :], c_low[rows, :] = halves(total)


def source_kernel(core, mine, theirs, b1_high, b1_low, out):
    first = core[0] == 0
    half = out.shape[0]
    start = pl.multiple_of(core[0] * half, half)
    a, b = mine[pl.ds(start, half), :], theirs[pl.ds(start, half), :]
    r0, r1 = jnp.where(first, a, b), jnp.where(first, b, a)
    out[...] = r1 + r0 + split_dot(r0, b1_high[...], b1_low[...])


def squares_kernel(counted, mine, theirs, out):
    def tile(ref):
        total = jnp.zeros((8, ref.shape[1]), F32)
        for at in range(0, ref.shape[0], 8):
            total = total + ref[at : at + 8, :] * ref[at : at + 8, :]
        return sum(total[:, at : at + 128] for at in range(0, ref.shape[1], 128))

    zero = jnp.zeros(out.shape, F32)
    a = jnp.where(counted[0] == 1, tile(mine), zero)
    out[...] = a + jnp.where(counted[1] == 1, tile(theirs), zero)


def hop_kernel(chunk, active, received, before, source, c_high, c_low, sent, kept):
    rows = received.shape[0]
    mine = active[0] == 1

    @pl.when(mine)
    def _():
        e = received[...]
        kept[...] = e
        sent[...] = e + source[chunk * rows : (chunk + 1) * rows, :] + split_dot(e, c_high[...], c_low[...])

    @pl.when(jnp.logical_not(mine))
    def _():
        kept[...] = before[...]


def finish_kernel(core, own, other, r_other, b0_high, b0_low, b1_high, b1_low, w, c, state, u):
    half = own.shape[0]

    def rest(e):
        step = e + split_dot(e, b0_high[...], b0_low[...])

        @pl.when(core[0] == 0)
        def _():
            state[...] = w[...] + step
            u[...] = c[...] + e

        @pl.when(core[0] == 1)
        def _():
            x = step + r_other[...]
            u[...] = c[...] + x
            state[...] = w[...] + (x + split_dot(x, b1_high[...], b1_low[...]))

    first = core[0] == 0
    mine, theirs = own[...], other[...]
    rest(jnp.concatenate([jnp.where(first, mine, theirs), jnp.where(first, theirs, mine)], 0))


def per_device(c_states, w_query, w_key, w_value, w_out):
    c_guess = c_states[0]
    dev_index = lax.axis_index("depth")
    dev_count = lax.axis_size("depth")
    chips = dev_count // 2
    chip = dev_index // 2
    core = jnp.reshape(dev_index % 2, (1,)).astype(jnp.int32)
    tokens, width = c_guess.shape
    half = tokens // 2
    rows = half // CHUNKS
    swap_pairs = [(i, i ^ 1) for i in range(dev_count)]

    def swap(block):
        return lax.ppermute(block, "depth", swap_pairs)

    def f32_of(*shape):
        return pltpu.VMEM(shape, F32)

    square = pltpu.VMEM((width, width), BF)
    next_state = lax.ppermute(c_guess, "depth", [(i, i - 1) for i in range(1, dev_count)])
    own_map = 0.25 * jnp.dot(w_value[1], w_out[1], preferred_element_type=F32)
    other_map = swap(own_map)
    fine_f = apply_layer(c_guess, w_query[0], w_key[0], w_value[0], w_out[0])
    fine_c = apply_layer(fine_f, w_query[1], w_key[1], w_value[1], w_out[1])
    residual = fine_c - next_state

    own_map, other_map = in_vmem(own_map, other_map)
    maps = call(parts_kernel, (square,) * 4, 3, 1 << 22)(core, own_map, other_map)
    b0_high, b0_low, b1_high, b1_low = in_vmem(*maps)
    other_residual = swap(residual)
    source = call(source_kernel, f32_of(half, width), 5, 6 * half * width * width)(
        core, residual, other_residual, b1_high, b1_low
    )
    c_high, c_low = in_vmem(
        *call(product_kernel, (square,) * 2, 7, 6 * width**3)(
            core, own_map, other_map, b0_high, b0_low, b1_high, b1_low
        )
    )

    sent = [source[j * rows : (j + 1) * rows] for j in range(CHUNKS)]
    (source,) = in_vmem(source)
    kept = [jnp.zeros((rows, width), F32)] * CHUNKS
    flags = jnp.stack([dev_index, dev_index ^ 1]) < dev_count - 1
    flags = flags.astype(jnp.int32)
    for hop in range(chips - 1):
        if hop == 3:
            flags, sent[-1] = lax.optimization_barrier((flags, sent[-1]))
            total = call(squares_kernel, pltpu.VMEM((8, 128), F32), 3, 1 << 20)(flags, residual, other_residual)
            kept[0], total = lax.optimization_barrier((kept[0], total))
        if hop >= 4 and hop % 2 == 0 and 2 << (hop // 2 - 2) < dev_count:
            reach = 2 << (hop // 2 - 2)
            total, sent[-1] = lax.optimization_barrier((total, sent[-1]))
            total = total + lax.ppermute(total, "depth", [(i, i ^ reach) for i in range(dev_count)])
            kept[0], total = lax.optimization_barrier((kept[0], total))
        pairs = [(2 * hop + i, 2 * hop + 2 + i) for i in range(2)]
        active = jnp.reshape((chip == hop + 1).astype(jnp.int32), (1,))
        for j in range(CHUNKS):
            received = lax.ppermute(sent[j], "depth", pairs)
            if hop < chips - 2:
                sent[j], kept[j] = call(
                    functools.partial(hop_kernel, j),
                    (f32_of(rows, width), f32_of(rows, width)),
                    6,
                    6 * rows * width * width,
                )(active, received, kept[j], source, c_high, c_low)
            else:
                kept[j] = jnp.where(active[0] == 1, received, kept[j])
    own_e = jnp.concatenate(kept, 0)
    other_e = swap(own_e)
    new_state, corrected = call(
        finish_kernel, (f32_of(tokens, width), f32_of(tokens, width)), 10, 12 * tokens * width * width
    )(core, own_e, other_e, other_residual, b0_high, b0_low, b1_high, b1_low, fine_c, c_guess)
    relaxed = apply_layer(corrected, w_query[0], w_key[0], w_value[0], w_out[0])
    residual_rms = jnp.sqrt(jnp.sum(total) / ((dev_count - 1) * tokens * width)).reshape(1)
    return (jnp.stack([relaxed, new_state]), residual_rms)


def solution(mesh):
    in_specs = (
        P("depth", "dp", None),
        P("depth", None, None),
        P("depth", None, None),
        P("depth", None, None),
        P("depth", None, None),
    )
    out_specs = (P("depth", "dp", None), P("dp"))
    return jax.shard_map(
        per_device, mesh=mesh, in_specs=in_specs, out_specs=out_specs, check_vma=False
    )
```

```python
import functools

import jax
import jax.numpy as jnp
from jax import lax
from jax.experimental import pallas as pl
from jax.experimental.pallas import tpu as pltpu
from jax.sharding import PartitionSpec as P

HEADS = 8
HEAD_DIM = 128
INNER = 1024
CHUNKS = 4
SHARED = 7

BF = jnp.bfloat16
F32 = jnp.float32
IN_VMEM = pl.BlockSpec(memory_space=pltpu.VMEM)
IN_SMEM = pl.BlockSpec(memory_space=pltpu.SMEM)


def normalize_rows(state):
    row_mean = jnp.mean(state, axis=-1, keepdims=True)
    centred = state - row_mean
    row_var = jnp.mean(centred * centred, axis=-1, keepdims=True)
    return centred * lax.rsqrt(row_var + 1e-05)


def apply_layer(state, w_query, w_key, w_value, w_out):
    tokens = state.shape[0]
    normed = normalize_rows(state).astype(jnp.bfloat16)
    query_rows = jnp.dot(normed, w_query, preferred_element_type=jnp.float32).astype(jnp.bfloat16)
    key_rows = jnp.dot(normed, w_key, preferred_element_type=jnp.float32).astype(jnp.bfloat16)
    value_rows = jnp.dot(normed, w_value, preferred_element_type=jnp.float32).astype(jnp.bfloat16)
    query_heads = query_rows.reshape(tokens, HEADS, HEAD_DIM)
    key_heads = key_rows.reshape(tokens, HEADS, HEAD_DIM)
    value_heads = value_rows.reshape(tokens, HEADS, HEAD_DIM)
    scores = jnp.einsum(
        "qhd,khd->hqk", query_heads, key_heads, preferred_element_type=jnp.float32
    ) * HEAD_DIM ** (-0.5)
    attn_probs = jax.nn.softmax(scores, axis=-1).astype(jnp.bfloat16)
    context = jnp.einsum(
        "hqk,khd->qhd", attn_probs, value_heads, preferred_element_type=jnp.float32
    )
    context = context.reshape(tokens, INNER).astype(jnp.bfloat16)
    return state + jnp.dot(context, w_out, preferred_element_type=jnp.float32)


def halves(value):
    high = value.astype(BF)
    return high, (value - high.astype(F32)).astype(BF)


def split_dot(left, right_high, right_low):
    rows = left.shape[0]
    high, low = halves(left)
    both = jnp.dot(jnp.concatenate([high, low], 0), right_high, preferred_element_type=F32)
    return both[:rows] + both[rows:] + jnp.dot(high, right_low, preferred_element_type=F32)


def in_vmem(*arrays):
    return tuple(pltpu.with_memory_space_constraint(a, pltpu.VMEM) for a in arrays)


def call(kernel, outs, n_in, flops, limit=40):
    return pl.pallas_call(
        kernel,
        out_shape=outs,
        in_specs=[IN_SMEM] + [IN_VMEM] * (n_in - 1),
        out_specs=jax.tree.map(lambda _: IN_VMEM, outs),
        compiler_params=pltpu.CompilerParams(vmem_limit_bytes=limit << 20),
        cost_estimate=pl.CostEstimate(flops=flops, bytes_accessed=1 << 20, transcendentals=0),
    )


def parts_kernel(core, own, other, b0_high, b0_low, b1_high, b1_low):
    first = core[0] == 0

    @pl.loop(0, own.shape[0] // 128)
    def _(block):
        rows = pl.ds(pl.multiple_of(block * 128, 128), 128)
        mine, theirs = own[rows, :], other[rows, :]
        b0_high[rows, :], b0_low[rows, :] = halves(jnp.where(first, mine, theirs))
        b1_high[rows, :], b1_low[rows, :] = halves(jnp.where(first, theirs, mine))


def product_kernel(core, own, other, b0_high, b0_low, b1_high, b1_low, c_high, c_low):
    @pl.loop(0, own.shape[0] // 256)
    def _(block):
        rows = pl.ds(pl.multiple_of(block * 256, 256), 256)
        high, low = b0_high[rows, :], b0_low[rows, :]
        both = jnp.dot(jnp.concatenate([high, low], 0), b1_high[...], preferred_element_type=F32)
        total = both[:256] + both[256:] + jnp.dot(high, b1_low[...], preferred_element_type=F32)
        total = total + (own[rows, :] + other[rows, :])
        c_high[rows, :], c_low[rows, :] = halves(total)


def source_kernel(core, mine, theirs, b1_high, b1_low, out):
    first = core[0] == 0
    half = out.shape[0]
    start = pl.multiple_of(core[0] * half, half)
    a, b = mine[pl.ds(start, half), :], theirs[pl.ds(start, half), :]
    r0, r1 = jnp.where(first, a, b), jnp.where(first, b, a)
    out[...] = r1 + r0 + split_dot(r0, b1_high[...], b1_low[...])


def squares_kernel(counted, mine, theirs, out):
    def tile(ref):
        total = jnp.zeros((8, ref.shape[1]), F32)
        for at in range(0, ref.shape[0], 8):
            total = total + ref[at : at + 8, :] * ref[at : at + 8, :]
        return sum(total[:, at : at + 128] for at in range(0, ref.shape[1], 128))

    zero = jnp.zeros(out.shape, F32)
    a = jnp.where(counted[0] == 1, tile(mine), zero)
    out[...] = a + jnp.where(counted[1] == 1, tile(theirs), zero)


def hop_kernel(chunk, active, received, before, source, c_high, c_low, sent, kept):
    rows = received.shape[0]
    mine = active[0] == 1

    @pl.when(mine)
    def _():
        e = received[...]
        kept[...] = e
        sent[...] = e + source[chunk * rows : (chunk + 1) * rows, :] + split_dot(e, c_high[...], c_low[...])

    @pl.when(jnp.logical_not(mine))
    def _():
        kept[...] = before[...]


def finish_kernel(core, own, other, r_other, b0_high, b0_low, b1_high, b1_low, w, c, state, u):
    half = own.shape[0]

    def rest(e):
        step = e + split_dot(e, b0_high[...], b0_low[...])

        @pl.when(core[0] == 0)
        def _():
            state[...] = w[...] + step
            u[...] = c[...] + e

        @pl.when(core[0] == 1)
        def _():
            x = step + r_other[...]
            u[...] = c[...] + x
            state[...] = w[...] + (x + split_dot(x, b1_high[...], b1_low[...]))

    first = core[0] == 0
    mine, theirs = own[...], other[...]
    rest(jnp.concatenate([jnp.where(first, mine, theirs), jnp.where(first, theirs, mine)], 0))


def per_device(c_states, w_query, w_key, w_value, w_out):
    c_guess = c_states[0]
    dev_index = lax.axis_index("depth")
    dev_count = lax.axis_size("depth")
    chips = dev_count // 2
    chip = dev_index // 2
    core = jnp.reshape(dev_index % 2, (1,)).astype(jnp.int32)
    tokens, width = c_guess.shape
    half = tokens // 2
    rows = half // CHUNKS
    swap_pairs = [(i, i ^ 1) for i in range(dev_count)]

    def swap(block):
        return lax.ppermute(block, "depth", swap_pairs)

    def f32_of(*shape):
        return pltpu.VMEM(shape, F32)

    square = pltpu.VMEM((width, width), BF)
    next_state = lax.ppermute(c_guess, "depth", [(i, i - 1) for i in range(1, dev_count)])
    own_map = 0.25 * jnp.dot(w_value[1], w_out[1], preferred_element_type=F32)
    other_map = swap(own_map)
    fine_f = apply_layer(c_guess, w_query[0], w_key[0], w_value[0], w_out[0])
    fine_c = apply_layer(fine_f, w_query[1], w_key[1], w_value[1], w_out[1])
    residual = fine_c - next_state

    own_map, other_map = in_vmem(own_map, other_map)
    maps = call(parts_kernel, (square,) * 4, 3, 1 << 22)(core, own_map, other_map)
    b0_high, b0_low, b1_high, b1_low = in_vmem(*maps)
    other_residual = swap(residual)
    source = call(source_kernel, f32_of(half, width), 5, 6 * half * width * width)(
        core, residual, other_residual, b1_high, b1_low
    )
    c_high, c_low = in_vmem(
        *call(product_kernel, (square,) * 2, 7, 6 * width**3)(
            core, own_map, other_map, b0_high, b0_low, b1_high, b1_low
        )
    )

    sent = [source[j * rows : (j + 1) * rows] for j in range(CHUNKS)]
    (source,) = in_vmem(source)
    kept = [jnp.zeros((rows, width), F32)] * CHUNKS
    flags = jnp.stack([dev_index, dev_index ^ 1]) < dev_count - 1
    flags = flags.astype(jnp.int32)
    for hop in range(chips - 1):
        if hop == 3:
            flags, sent[-1] = lax.optimization_barrier((flags, sent[-1]))
            total = call(squares_kernel, pltpu.VMEM((8, 128), F32), 3, 1 << 20)(flags, residual, other_residual)
            kept[0], total = lax.optimization_barrier((kept[0], total))
        if hop >= 4 and hop % 2 == 0 and 2 << (hop // 2 - 2) < dev_count:
            reach = 2 << (hop // 2 - 2)
            total, sent[-1] = lax.optimization_barrier((total, sent[-1]))
            total = total + lax.ppermute(total, "depth", [(i, i ^ reach) for i in range(dev_count)])
            kept[0], total = lax.optimization_barrier((kept[0], total))
        pairs = [
            (2 * at + i, 2 * at + 2 + i) for at in range(hop % SHARED, chips - 1, SHARED) for i in range(2)
        ]
        active = jnp.reshape((chip == hop + 1).astype(jnp.int32), (1,))
        for j in range(CHUNKS):
            received = lax.ppermute(sent[j], "depth", pairs)
            if hop < chips - 2:
                sent[j], kept[j] = call(
                    functools.partial(hop_kernel, j),
                    (f32_of(rows, width), f32_of(rows, width)),
                    6,
                    6 * rows * width * width,
                )(active, received, kept[j], source, c_high, c_low)
            else:
                kept[j] = jnp.where(active[0] == 1, received, kept[j])
    own_e = jnp.concatenate(kept, 0)
    other_e = swap(own_e)
    new_state, corrected = call(
        finish_kernel, (f32_of(tokens, width), f32_of(tokens, width)), 10, 12 * tokens * width * width
    )(core, own_e, other_e, other_residual, b0_high, b0_low, b1_high, b1_low, fine_c, c_guess)
    relaxed = apply_layer(corrected, w_query[0], w_key[0], w_value[0], w_out[0])
    residual_rms = jnp.sqrt(jnp.sum(total) / ((dev_count - 1) * tokens * width)).reshape(1)
    return (jnp.stack([relaxed, new_state]), residual_rms)


def solution(mesh):
    in_specs = (
        P("depth", "dp", None),
        P("depth", None, None),
        P("depth", None, None),
        P("depth", None, None),
        P("depth", None, None),
    )
    out_specs = (P("depth", "dp", None), P("dp"))
    return jax.shard_map(
        per_device, mesh=mesh, in_specs=in_specs, out_specs=out_specs, check_vma=False
    )
```

```python
import functools

import jax
import jax.numpy as jnp
from jax import lax
from jax.experimental import pallas as pl
from jax.experimental.pallas import tpu as pltpu
from jax.sharding import PartitionSpec as P

HEADS = 8
HEAD_DIM = 128
INNER = 1024
CHUNKS = 4
SHARED = 6
TILE = 256
UNROLL = True
HOP_TILE = 256

BF = jnp.bfloat16
F32 = jnp.float32
IN_VMEM = pl.BlockSpec(memory_space=pltpu.VMEM)
IN_SMEM = pl.BlockSpec(memory_space=pltpu.SMEM)
IN_PLACE = pl.BlockSpec(memory_space=pltpu.HBM)


def dot(left, right):
    return jnp.dot(left, right, preferred_element_type=F32)


def tiles(width, tile, body, unroll):
    if unroll:
        for at in range(0, width, tile):
            body(pl.ds(at, tile))
    else:
        pl.loop(0, width // tile)(lambda i: body(pl.ds(pl.multiple_of(i * tile, tile), tile)))


def halves(value):
    high = value.astype(BF)
    return high, (value - high.astype(F32)).astype(BF)


def split_dot(left, right):
    rows = left.shape[0]
    both = dot(jnp.concatenate(halves(left), 0), right)
    return both[:rows] + both[rows:]


def in_vmem(*arrays):
    return tuple(pltpu.with_memory_space_constraint(a, pltpu.VMEM) for a in arrays)


def call(kernel, outs, specs, flops, limit=8, scratch=(), out_specs=None, aliases=None):
    return pl.pallas_call(
        kernel,
        out_shape=outs,
        in_specs=specs,
        out_specs=out_specs or jax.tree.map(lambda _: IN_VMEM, outs),
        scratch_shapes=scratch,
        input_output_aliases=aliases or {},
        compiler_params=pltpu.CompilerParams(vmem_limit_bytes=limit << 20),
        cost_estimate=pl.CostEstimate(flops=flops, bytes_accessed=1 << 20, transcendentals=0),
    )


def layer(state, query, key, value, out_map, waits, normed, context, result):
    rows = state[...]
    centred = rows - jnp.mean(rows, axis=-1, keepdims=True)
    row_var = jnp.mean(centred * centred, axis=-1, keepdims=True)
    normed[...] = (centred * lax.rsqrt(row_var + 1e-05)).astype(BF)
    for wait in waits[:3]:
        wait()

    def heads(cols):
        n = normed[...]
        q = dot(n, query[:, cols]).astype(BF)
        k = dot(n, key[:, cols]).astype(BF)
        v = dot(n, value[:, cols]).astype(BF)
        parts = []
        for at in range(0, TILE, HEAD_DIM):
            one = slice(at, at + HEAD_DIM)
            scores = lax.dot_general(
                q[:, one], k[:, one], (((1,), (1,)), ((), ())), preferred_element_type=F32
            ) * HEAD_DIM ** (-0.5)
            grown = jnp.exp(scores - jnp.max(scores, axis=-1, keepdims=True))
            share = 1.0 / jnp.sum(grown, axis=-1, keepdims=True)
            parts.append(dot((grown * share).astype(BF), v[:, one]).astype(BF))
        context[:, cols] = jnp.concatenate(parts, 1)

    tiles(INNER, TILE, heads, UNROLL)
    waits[3]()

    def project(cols):
        result[:, cols] = state[:, cols] + dot(context[...], out_map[:, cols])

    tiles(state.shape[1], TILE, project, UNROLL)


def maps_kernel(place, w_query, w_key, w_value, w_out, own, own_high, query, key, value, v1, o1, sems):
    moves = [
        pltpu.make_async_copy(src.at[at], dst, sems.at[i])
        for i, (src, at, dst) in enumerate(
            [(w_value, 1, v1), (w_out, 1, o1), (w_query, 0, query), (w_key, 0, key), (w_value, 0, value)]
        )
    ]
    for move in moves:
        move.start()
    moves[0].wait()
    moves[1].wait()

    @pl.loop(0, own.shape[0] // 256)
    def _(block):
        rows = pl.ds(pl.multiple_of(block * 256, 256), 256)
        product = 0.25 * dot(v1[rows, :], o1[...])
        own[rows, :] = product
        own_high[rows, :] = product.astype(BF)

    for move in moves[2:]:
        move.wait()


def advance_kernel(
    c, query, key, value, w_query, w_key, w_value, w_out, out, o0, q1, k1, v1, o1, middle, normed, context, sems
):
    moves = [
        pltpu.make_async_copy(src.at[at], dst, sems.at[i])
        for i, (src, at, dst) in enumerate(
            [(w_out, 0, o0), (w_query, 1, q1), (w_key, 1, k1), (w_value, 1, v1), (w_out, 1, o1)]
        )
    ]
    for move in moves:
        move.start()
    here = lambda: None
    layer(c, query, key, value, o0, [here, here, here, moves[0].wait], normed, context, middle)
    layer(middle, q1, k1, v1, o1, [move.wait for move in moves[1:]], normed, context, out)


def subtract_kernel(left, right, out):
    out[...] = left[...] - right[...]


def cast_kernel(wide, out):
    @pl.loop(0, wide.shape[0] // 128)
    def _(block):
        rows = pl.ds(pl.multiple_of(block * 128, 128), 128)
        out[rows, :] = wide[rows, :].astype(BF)


def add_kernel(left, right, out):
    out[...] = left[...] + right[...]


def product_kernel(place, own, other, own_high, other_high, c_high):
    def body(first, second):
        @pl.loop(0, own.shape[0] // 256)
        def _(block):
            rows = pl.ds(pl.multiple_of(block * 256, 256), 256)
            for at in range(0, own.shape[1], 256):
                cols = slice(at, at + 256)
                total = dot(first[rows, :], second[:, cols]) + (own[rows, cols] + other[rows, cols])
                c_high[rows, cols] = total.astype(BF)

    pl.when(place[0] == 0)(lambda: body(own_high, other_high))
    pl.when(place[0] == 1)(lambda: body(other_high, own_high))


def source_kernel(place, mine, theirs, own_high, other_high, r0_half, *out):
    half = r0_half.shape[0]
    rows = half // CHUNKS

    def body(r0, r1, at, high):
        r0_half[...] = r0[at : at + half, :]
        total = r1[at : at + half, :] + r0[at : at + half, :] + split_dot(r0[at : at + half, :], high[...])
        for j in range(CHUNKS):
            out[j][...] = total[j * rows : (j + 1) * rows]

    pl.when(place[0] == 0)(lambda: body(mine, theirs, 0, other_high))
    pl.when(place[0] == 1)(lambda: body(theirs, mine, half, own_high))


def squares_kernel(place, mine, theirs, out):
    def tile(ref):
        def body(at, total):
            rows = ref[pl.ds(pl.multiple_of(at * 8, 8), 8), :]
            return total + rows * rows

        total = lax.fori_loop(0, ref.shape[0] // 8, body, jnp.zeros((8, ref.shape[1]), F32))
        return sum(total[:, at : at + 128] for at in range(0, ref.shape[1], 128))

    zero = jnp.zeros(out.shape, F32)
    a = jnp.where(place[2] == 1, tile(mine), zero)
    out[...] = a + jnp.where(place[3] == 1, tile(theirs), zero)


def times_chunk(e, matrix, body, tile=HOP_TILE, unroll=True):
    rows = e.shape[0]
    both = jnp.concatenate(halves(e), 0)

    def part(cols):
        wide = dot(both, matrix[:, cols])
        body(cols, wide[:rows] + wide[rows:])

    tiles(matrix.shape[1], tile, part, unroll)


def hop_kernel(hop, place, received, *refs):
    source, c_high, sent, kept = refs[-4:]
    if hop == 0:
        kept[...] = jnp.zeros_like(kept)

    @pl.when(place[1] == hop + 1)
    def _():
        kept[...] = received[...]

        def body(cols, product):
            sent[:, cols] = received[:, cols] + source[:, cols] + product

        times_chunk(received[...], c_high, body)


def last_kernel(chunk, hop, place, received, before, r0_half, own_high, other_high, mine, sent):
    rows = received.shape[0]

    def body(kept, first, second, high):
        first[...] = kept

        def part(cols, product):
            second[:, cols] = (
                first[:, cols] + product + r0_half[chunk * rows : (chunk + 1) * rows, cols]
            )

        times_chunk(kept, high, part)

    e = jnp.where(place[1] == hop + 1, received[...], before[...])
    pl.when(place[0] == 0)(lambda: body(e, mine, sent, own_high))
    pl.when(place[0] == 1)(lambda: body(e, sent, mine, other_high))


def finish_kernel(count, place, *refs):
    mine, theirs = refs[:CHUNKS], refs[CHUNKS : 2 * CHUNKS]
    own_high, w, c, total, w_query, w_key, w_value, w_out, out, rms = refs[2 * CHUNKS : 2 * CHUNKS + 10]
    q0, k0, v0, o0, x, u, result, normed, context, sems = refs[2 * CHUNKS + 10 :]
    moves = [
        pltpu.make_async_copy(src.at[0], dst, sems.at[i])
        for i, (src, dst) in enumerate([(w_query, q0), (w_key, k0), (w_value, v0), (w_out, o0)])
    ]
    for move in moves:
        move.start()
    rows = mine[0].shape[0]
    half = rows * CHUNKS

    def gather(low, high):
        for j in range(CHUNKS):
            x[j * rows : (j + 1) * rows, :] = low[j][...]
            x[half + j * rows : half + (j + 1) * rows, :] = high[j][...]

    pl.when(place[0] == 0)(lambda: gather(mine, theirs))
    pl.when(place[0] == 1)(lambda: gather(theirs, mine))
    u[...] = c[...] + x[...]

    def carry(cols, product):
        result[1, :, cols] = w[:, cols] + x[:, cols] + product

    times_chunk(x[...], own_high, carry)
    mean_sq = jnp.sum(total[...], keepdims=True) / count
    rms[0] = jnp.sqrt(mean_sq)[0, 0]
    second = pltpu.make_async_copy(result.at[1], out.at[1], sems.at[4])
    second.start()
    layer(u, q0, k0, v0, o0, [move.wait for move in moves], normed, context, result.at[0])
    first = pltpu.make_async_copy(result.at[0], out.at[0], sems.at[5])
    first.start()
    first.wait()
    second.wait()


def per_device(c_states, w_query, w_key, w_value, w_out):
    c_guess = c_states[0]
    dev_index = lax.axis_index("depth")
    dev_count = lax.axis_size("depth")
    chips = dev_count // 2
    chip = dev_index // 2
    core = dev_index % 2
    place = [core, chip, dev_index < dev_count - 1, dev_index - core < dev_count - 2 + core]
    place = jnp.stack([jnp.asarray(item, jnp.int32) for item in place])
    tokens, width = c_guess.shape
    half = tokens // 2
    rows = half // CHUNKS
    swap_pairs = [(i, i ^ 1) for i in range(dev_count)]
    dma = pltpu.SemaphoreType.DMA

    def swap(block):
        return lax.ppermute(block, "depth", swap_pairs)

    def f32_of(*shape):
        return pltpu.VMEM(shape, F32)

    def bf_of(*shape):
        return pltpu.VMEM(shape, BF)

    square = bf_of(width, width)
    state = f32_of(tokens, width)
    chunk = f32_of(rows, width)
    thin = bf_of(tokens, width)

    w_query, w_key, w_value, w_out = (
        pltpu.with_memory_space_constraint(w, pltpu.HBM) for w in (w_query, w_key, w_value, w_out)
    )
    next_state = lax.ppermute(c_guess, "depth", [(i, i - 1) for i in range(1, dev_count)])
    own, own_high, query, key, value = call(
        maps_kernel,
        (f32_of(width, width),) + (square,) * 4,
        [IN_SMEM] + [IN_PLACE] * 4,
        2 * width**3,
        limit=16,
        scratch=[square, square, dma((5,))],
    )(place, w_query, w_key, w_value, w_out)
    other = swap(own)
    query, key, value, c_guess = in_vmem(query, key, value, c_guess)
    fine_c = call(
        advance_kernel,
        state,
        [IN_VMEM] * 4 + [IN_PLACE] * 4,
        20 * tokens * width * width,
        limit=28,
        scratch=[square] * 5 + [state, thin, thin, dma((5,))],
    )(c_guess, query, key, value, w_query, w_key, w_value, w_out)
    fine_c, next_state = in_vmem(fine_c, next_state)
    residual = call(subtract_kernel, state, [IN_VMEM] * 2, 1 << 18, limit=4)(fine_c, next_state)
    other_residual = swap(residual)
    own, other, own_high = in_vmem(own, other, own_high)
    other_high, residual, other_residual = in_vmem(
        call(cast_kernel, square, [IN_VMEM], 1 << 20, limit=4)(other), residual, other_residual
    )
    r0_half, *source = call(
        source_kernel,
        (f32_of(half, width),) + (chunk,) * CHUNKS,
        [IN_SMEM] + [IN_VMEM] * 4,
        4 * half * width * width,
    )(place, residual, other_residual, own_high, other_high)
    (c_high,) = in_vmem(
        call(product_kernel, square, [IN_SMEM] + [IN_VMEM] * 4, 2 * width**3, limit=16)(
            place, own, other, own_high, other_high
        )
    )

    sent = list(source)
    source = in_vmem(*source)
    kept = [None] * CHUNKS
    for hop in range(chips - 1):
        if hop == 3:
            residual, sent[-1] = lax.optimization_barrier((residual, sent[-1]))
            (residual,) = in_vmem(residual)
            total = call(squares_kernel, f32_of(8, 128), [IN_SMEM, IN_VMEM, IN_VMEM], 1 << 20, limit=4)(
                place, residual, other_residual
            )
            kept[0], total = lax.optimization_barrier((kept[0], total))
        if hop >= 4 and hop % 2 == 0 and 2 << (hop // 2 - 2) < dev_count:
            reach = 2 << (hop // 2 - 2)
            total, sent[-1] = lax.optimization_barrier((total, sent[-1]))
            theirs = lax.ppermute(total, "depth", [(i, i ^ reach) for i in range(dev_count)])
            total = call(add_kernel, f32_of(8, 128), [IN_VMEM] * 2, 1 << 12, limit=4)(total, theirs)
            kept[0], total = lax.optimization_barrier((kept[0], total))
        pairs = [
            (2 * at + i, 2 * at + 2 + i) for at in range(hop % SHARED, chips - 1, SHARED) for i in range(2)
        ]
        for j in range(CHUNKS):
            received = lax.ppermute(sent[j], "depth", pairs)
            held = in_vmem(received) if hop == 0 else in_vmem(received, kept[j])
            if hop < chips - 2:
                sent[j], kept[j] = call(
                    functools.partial(hop_kernel, hop),
                    (chunk, chunk),
                    [IN_SMEM] + [IN_VMEM] * (len(held) + 2),
                    4 * rows * width * width,
                    limit=4,
                    aliases={2: 1} if hop else None,
                )(place, *held, source[j], c_high)
            else:
                kept[j], sent[j] = call(
                    functools.partial(last_kernel, j, hop),
                    (chunk, chunk),
                    [IN_SMEM] + [IN_VMEM] * 5,
                    4 * rows * width * width,
                    limit=4,
                )(place, *held, r0_half, own_high, other_high)
    crossed = in_vmem(*[swap(block) for block in sent])
    kept = in_vmem(*kept)
    (fine_c,) = in_vmem(fine_c)
    return call(
        functools.partial(finish_kernel, float((dev_count - 1) * tokens * width)),
        (jax.ShapeDtypeStruct((2, tokens, width), F32), jax.ShapeDtypeStruct((1,), F32)),
        [IN_SMEM] + [IN_VMEM] * (2 * CHUNKS + 4) + [IN_PLACE] * 4,
        18 * tokens * width * width,
        limit=28,
        scratch=[square] * 4 + [state, state, f32_of(2, tokens, width), thin, thin, dma((6,))],
        out_specs=(IN_PLACE, IN_SMEM),
    )(place, *kept, *crossed, own_high, fine_c, c_guess, total, w_query, w_key, w_value, w_out)


def solution(mesh):
    in_specs = (
        P("depth", "dp", None),
        P("depth", None, None),
        P("depth", None, None),
        P("depth", None, None),
        P("depth", None, None),
    )
    out_specs = (P("depth", "dp", None), P("dp"))
    return jax.shard_map(
        per_device, mesh=mesh, in_specs=in_specs, out_specs=out_specs, check_vma=False
    )
```

```python
import functools

import jax
import jax.numpy as jnp
from jax import lax
from jax.experimental import pallas as pl
from jax.experimental.pallas import tpu as pltpu
from jax.sharding import PartitionSpec as P

HEADS = 8
HEAD_DIM = 128
INNER = 1024
CHUNKS = 4
GROUPS = ((0, 1, 2, 3, 4), (0, 3, 1, 4, 2), (1, 2, 0, 4, 3))
ROUNDS = {4: 16, 9: 8, 11: 4, 13: 2}
TILE = 256
UNROLL = True
HOP_TILE = 256

BF = jnp.bfloat16
F32 = jnp.float32
IN_VMEM = pl.BlockSpec(memory_space=pltpu.VMEM)
IN_SMEM = pl.BlockSpec(memory_space=pltpu.SMEM)
IN_PLACE = pl.BlockSpec(memory_space=pltpu.HBM)


def dot(left, right):
    return jnp.dot(left, right, preferred_element_type=F32)


def on_core(core):
    return lax.axis_index("depth") % 2 == core


def on_chip(chip):
    return lax.axis_index("depth") // 2 == chip


def group_of(hop):
    part, at = divmod(hop, len(GROUPS[0]))
    return GROUPS[part % len(GROUPS)][at]


def tiles(width, tile, body, unroll):
    if unroll:
        for at in range(0, width, tile):
            body(pl.ds(at, tile))
    else:
        pl.loop(0, width // tile)(lambda i: body(pl.ds(pl.multiple_of(i * tile, tile), tile)))


def halves(value):
    high = value.astype(BF)
    return high, (value - high.astype(F32)).astype(BF)


def split_dot(left, right):
    rows = left.shape[0]
    both = dot(jnp.concatenate(halves(left), 0), right)
    return both[:rows] + both[rows:]


def in_vmem(*arrays):
    return tuple(pltpu.with_memory_space_constraint(a, pltpu.VMEM) for a in arrays)


def call(kernel, outs, specs, flops, limit=8, scratch=(), out_specs=None, aliases=None):
    return pl.pallas_call(
        kernel,
        out_shape=outs,
        in_specs=specs,
        out_specs=out_specs or jax.tree.map(lambda _: IN_VMEM, outs),
        scratch_shapes=scratch,
        input_output_aliases=aliases or {},
        compiler_params=pltpu.CompilerParams(vmem_limit_bytes=limit << 20),
        cost_estimate=pl.CostEstimate(flops=flops, bytes_accessed=1 << 20, transcendentals=0),
    )


def layer(state, query, key, value, out_map, waits, normed, context, result):
    rows = state[...]
    centred = rows - jnp.mean(rows, axis=-1, keepdims=True)
    row_var = jnp.mean(centred * centred, axis=-1, keepdims=True)
    normed[...] = (centred * lax.rsqrt(row_var + 1e-05)).astype(BF)
    for wait in waits[:3]:
        wait()

    def heads(cols):
        n = normed[...]
        q = dot(n, query[:, cols]).astype(BF)
        k = dot(n, key[:, cols]).astype(BF)
        v = dot(n, value[:, cols]).astype(BF)
        parts = []
        for at in range(0, TILE, HEAD_DIM):
            one = slice(at, at + HEAD_DIM)
            scores = lax.dot_general(
                q[:, one], k[:, one], (((1,), (1,)), ((), ())), preferred_element_type=F32
            ) * HEAD_DIM ** (-0.5)
            grown = jnp.exp(scores - jnp.max(scores, axis=-1, keepdims=True))
            share = 1.0 / jnp.sum(grown, axis=-1, keepdims=True)
            parts.append(dot((grown * share).astype(BF), v[:, one]).astype(BF))
        context[:, cols] = jnp.concatenate(parts, 1)

    tiles(INNER, TILE, heads, UNROLL)
    waits[3]()

    def project(cols):
        result[:, cols] = state[:, cols] + dot(context[...], out_map[:, cols])

    tiles(state.shape[1], TILE, project, UNROLL)


def maps_kernel(w_query, w_key, w_value, w_out, own, own_high, query, key, value, v1, o1, sems):
    moves = [
        pltpu.make_async_copy(src.at[at], dst, sems.at[i])
        for i, (src, at, dst) in enumerate(
            [(w_value, 1, v1), (w_out, 1, o1), (w_query, 0, query), (w_key, 0, key), (w_value, 0, value)]
        )
    ]
    for move in moves:
        move.start()
    moves[0].wait()
    moves[1].wait()

    @pl.loop(0, own.shape[0] // 256)
    def _(block):
        rows = pl.ds(pl.multiple_of(block * 256, 256), 256)
        product = 0.25 * dot(v1[rows, :], o1[...])
        own[rows, :] = product
        own_high[rows, :] = product.astype(BF)

    for move in moves[2:]:
        move.wait()


def advance_kernel(
    c, query, key, value, w_query, w_key, w_value, w_out, out, o0, q1, k1, v1, o1, middle, normed, context, sems
):
    moves = [
        pltpu.make_async_copy(src.at[at], dst, sems.at[i])
        for i, (src, at, dst) in enumerate(
            [(w_out, 0, o0), (w_query, 1, q1), (w_key, 1, k1), (w_value, 1, v1), (w_out, 1, o1)]
        )
    ]
    for move in moves:
        move.start()
    here = lambda: None
    layer(c, query, key, value, o0, [here, here, here, moves[0].wait], normed, context, middle)
    layer(middle, q1, k1, v1, o1, [move.wait for move in moves[1:]], normed, context, out)


def subtract_kernel(left, right, out):
    out[...] = left[...] - right[...]


def cast_kernel(wide, out):
    @pl.loop(0, wide.shape[0] // 128)
    def _(block):
        rows = pl.ds(pl.multiple_of(block * 128, 128), 128)
        out[rows, :] = wide[rows, :].astype(BF)


def add_kernel(left, right, out):
    out[...] = left[...] + right[...]


def product_kernel(own, other, own_high, other_high, c_high, c_low):
    def body(first, second):
        @pl.loop(0, own.shape[0] // 256)
        def _(block):
            rows = pl.ds(pl.multiple_of(block * 256, 256), 256)
            for at in range(0, own.shape[1], 256):
                cols = slice(at, at + 256)
                total = dot(first[rows, :], second[:, cols]) + (own[rows, cols] + other[rows, cols])
                c_high[rows, cols], c_low[rows, cols] = halves(total)

    pl.when(on_core(0))(lambda: body(own_high, other_high))
    pl.when(on_core(1))(lambda: body(other_high, own_high))


def source_kernel(mine, theirs, own_high, other_high, r0_half, *out):
    half = r0_half.shape[0]
    rows = half // CHUNKS

    def body(r0, r1, at, high):
        r0_half[...] = r0[at : at + half, :]
        total = r1[at : at + half, :] + r0[at : at + half, :] + split_dot(r0[at : at + half, :], high[...])
        for j in range(CHUNKS):
            out[j][...] = total[j * rows : (j + 1) * rows]

    pl.when(on_core(0))(lambda: body(mine, theirs, 0, other_high))
    pl.when(on_core(1))(lambda: body(theirs, mine, half, own_high))


def squares_kernel(mine, theirs, out):
    def tile(ref):
        def body(at, total):
            rows = ref[pl.ds(pl.multiple_of(at * 8, 8), 8), :]
            return total + rows * rows

        total = lax.fori_loop(0, ref.shape[0] // 8, body, jnp.zeros((8, ref.shape[1]), F32))
        return sum(total[:, at : at + 128] for at in range(0, ref.shape[1], 128))

    last = lax.axis_size("depth") - 1
    me = lax.axis_index("depth")
    zero = jnp.zeros(out.shape, F32)
    a = jnp.where(me != last, tile(mine), zero)
    out[...] = a + jnp.where(me != last - 1, tile(theirs), zero)


def times_chunk(e, matrix, body, low=None):
    rows = e.shape[0]
    e_high, e_low = halves(e)
    both = jnp.concatenate([e_high, e_low], 0)

    def part(cols):
        wide = dot(both, matrix[:, cols])
        product = wide[:rows] + wide[rows:]
        body(cols, product if low is None else product + dot(e_high, low[:, cols]))

    tiles(matrix.shape[1], HOP_TILE, part, True)


def hop_kernel(hop, received, *refs):
    source, c_high, c_low, sent, kept = refs[-5:]

    @pl.when(on_chip(hop + 1))
    def _():
        kept[...] = received[...]

        def body(cols, product):
            sent[:, cols] = received[:, cols] + source[:, cols] + product

        times_chunk(received[...], c_high, body, c_low)

    @pl.when(jnp.logical_not(on_chip(hop + 1)))
    def _():
        kept[...] = jnp.zeros_like(kept) if hop == 0 else refs[0][...]


def last_kernel(chunk, hop, received, before, r0_half, own_high, other_high, mine, sent):
    rows = received.shape[0]

    def body(kept, first, second, high):
        first[...] = kept

        def part(cols, product):
            second[:, cols] = (
                first[:, cols] + product + r0_half[chunk * rows : (chunk + 1) * rows, cols]
            )

        times_chunk(kept, high, part)

    e = jnp.where(on_chip(hop + 1), received[...], before[...])
    pl.when(on_core(0))(lambda: body(e, mine, sent, own_high))
    pl.when(on_core(1))(lambda: body(e, sent, mine, other_high))


def finish_kernel(count, *refs):
    mine, theirs = refs[:CHUNKS], refs[CHUNKS : 2 * CHUNKS]
    own_high, w, c, total, q0, k0, v0, o0, out, rms = refs[2 * CHUNKS : 2 * CHUNKS + 10]
    x, u, result, normed, context, sems = refs[2 * CHUNKS + 10 :]
    rows = mine[0].shape[0]
    half = rows * CHUNKS

    def gather(low, high):
        for j in range(CHUNKS):
            x[j * rows : (j + 1) * rows, :] = low[j][...]
            x[half + j * rows : half + (j + 1) * rows, :] = high[j][...]

    pl.when(on_core(0))(lambda: gather(mine, theirs))
    pl.when(on_core(1))(lambda: gather(theirs, mine))
    u[...] = c[...] + x[...]

    def carry(cols, product):
        result[1, :, cols] = w[:, cols] + x[:, cols] + product

    times_chunk(x[...], own_high, carry)
    mean_sq = jnp.sum(total[...], keepdims=True) / count
    rms[0] = jnp.sqrt(mean_sq)[0, 0]
    second = pltpu.make_async_copy(result.at[1], out.at[1], sems.at[0])
    second.start()
    layer(u, q0, k0, v0, o0, [lambda: None] * 4, normed, context, result.at[0])
    first = pltpu.make_async_copy(result.at[0], out.at[0], sems.at[1])
    first.start()
    first.wait()
    second.wait()


def per_device(c_states, w_query, w_key, w_value, w_out):
    c_guess = c_states[0]
    dev_count = lax.axis_size("depth")
    chips = dev_count // 2
    tokens, width = c_guess.shape
    half = tokens // 2
    rows = half // CHUNKS
    swap_pairs = [(i, i ^ 1) for i in range(dev_count)]
    dma = pltpu.SemaphoreType.DMA

    def swap(block):
        return lax.ppermute(block, "depth", swap_pairs)

    def f32_of(*shape):
        return pltpu.VMEM(shape, F32)

    def bf_of(*shape):
        return pltpu.VMEM(shape, BF)

    square = bf_of(width, width)
    state = f32_of(tokens, width)
    chunk = f32_of(rows, width)
    thin = bf_of(tokens, width)

    w_query, w_key, w_value, w_out = (
        pltpu.with_memory_space_constraint(w, pltpu.HBM) for w in (w_query, w_key, w_value, w_out)
    )
    next_state = lax.ppermute(c_guess, "depth", [(i, i - 1) for i in range(1, dev_count)])
    own, own_high, query, key, value = call(
        maps_kernel,
        (f32_of(width, width),) + (square,) * 4,
        [IN_PLACE] * 4,
        2 * width**3,
        limit=16,
        scratch=[square, square, dma((5,))],
    )(w_query, w_key, w_value, w_out)
    other = swap(own)
    query, key, value, c_guess = in_vmem(query, key, value, c_guess)
    fine_c, out_map = call(
        advance_kernel,
        (state, square),
        [IN_VMEM] * 4 + [IN_PLACE] * 4,
        20 * tokens * width * width,
        limit=28,
        scratch=[square] * 4 + [state, thin, thin, dma((5,))],
    )(c_guess, query, key, value, w_query, w_key, w_value, w_out)
    fine_c, next_state = in_vmem(fine_c, next_state)
    residual = call(subtract_kernel, state, [IN_VMEM] * 2, 1 << 18, limit=4)(fine_c, next_state)
    other_residual = swap(residual)
    own, other, own_high = in_vmem(own, other, own_high)
    other_high, residual = in_vmem(
        call(cast_kernel, square, [IN_VMEM], 1 << 20, limit=4)(other), residual
    )
    c_high, c_low = call(product_kernel, (square, square), [IN_VMEM] * 4, 2 * width**3, limit=16)(
        own, other, own_high, other_high
    )
    other_residual, c_high = lax.optimization_barrier((other_residual, c_high))
    other_residual, c_high, c_low = in_vmem(other_residual, c_high, c_low)
    r0_half, *source = call(
        source_kernel,
        (f32_of(half, width),) + (chunk,) * CHUNKS,
        [IN_VMEM] * 4,
        4 * half * width * width,
    )(residual, other_residual, own_high, other_high)
    sent = list(source)
    source = in_vmem(*source)
    kept = [None] * CHUNKS
    for hop in range(chips - 1):
        if hop == 3:
            residual, sent[-1] = lax.optimization_barrier((residual, sent[-1]))
            (residual,) = in_vmem(residual)
            total = call(squares_kernel, f32_of(8, 128), [IN_VMEM] * 2, 1 << 20, limit=4)(
                residual, other_residual
            )
        if hop in ROUNDS:
            reach = ROUNDS[hop]
            total, sent[-1] = lax.optimization_barrier((total, sent[-1]))
            theirs = lax.ppermute(total, "depth", [(i, i ^ reach) for i in range(dev_count)])
            total = call(add_kernel, f32_of(8, 128), [IN_VMEM] * 2, 1 << 12, limit=4)(total, theirs)
            kept[0], total = lax.optimization_barrier((kept[0], total))
        alike = [at for at in range(chips - 1) if group_of(at) == group_of(hop)]
        pairs = [(2 * at + i, 2 * at + 2 + i) for at in alike for i in range(2)]
        for j in range(CHUNKS):
            received = lax.ppermute(sent[j], "depth", pairs)
            held = in_vmem(received) if hop == 0 else in_vmem(received, kept[j])
            if hop < chips - 2:
                sent[j], kept[j] = call(
                    functools.partial(hop_kernel, hop),
                    (chunk, chunk),
                    [IN_VMEM] * (len(held) + 3),
                    4 * rows * width * width,
                    limit=4,
                )(*held, source[j], c_high, c_low)
            else:
                kept[j], sent[j] = call(
                    functools.partial(last_kernel, j, hop),
                    (chunk, chunk),
                    [IN_VMEM] * 5,
                    4 * rows * width * width,
                    limit=4,
                )(*held, r0_half, own_high, other_high)
    crossed = in_vmem(*[swap(block) for block in sent])
    kept = in_vmem(*kept)
    (out_map,) = in_vmem(out_map)
    return call(
        functools.partial(finish_kernel, float((dev_count - 1) * tokens * width)),
        (jax.ShapeDtypeStruct((2, tokens, width), F32), jax.ShapeDtypeStruct((1,), F32)),
        [IN_VMEM] * (2 * CHUNKS + 8),
        18 * tokens * width * width,
        limit=20,
        scratch=[state, state, f32_of(2, tokens, width), thin, thin, dma((2,))],
        out_specs=(IN_PLACE, IN_SMEM),
    )(*kept, *crossed, own_high, fine_c, c_guess, total, query, key, value, out_map)


def solution(mesh):
    in_specs = (
        P("depth", "dp", None),
        P("depth", None, None),
        P("depth", None, None),
        P("depth", None, None),
        P("depth", None, None),
    )
    out_specs = (P("depth", "dp", None), P("dp"))
    return jax.shard_map(
        per_device, mesh=mesh, in_specs=in_specs, out_specs=out_specs, check_vma=False
    )
```

```python
import functools

import jax
import jax.numpy as jnp
from jax import lax
from jax.experimental import pallas as pl
from jax.experimental.pallas import tpu as pltpu
from jax.sharding import PartitionSpec as P

HEADS = 8
HEAD_DIM = 128
INNER = 1024
CHUNKS = 4
EXPONENT = HEAD_DIM ** (-0.5) * 1.4426950408889634
GROUPS = ((0, 1, 2, 3, 4), (0, 3, 1, 4, 2), (1, 2, 0, 4, 3))
ROUNDS = {4: 16, 9: 8, 11: 4, 13: 2}
TILE = 256
UNROLL = True
HOP_TILE = 256

BF = jnp.bfloat16
F32 = jnp.float32
IN_VMEM = pl.BlockSpec(memory_space=pltpu.VMEM)
IN_SMEM = pl.BlockSpec(memory_space=pltpu.SMEM)
IN_PLACE = pl.BlockSpec(memory_space=pltpu.HBM)


def dot(left, right):
    return jnp.dot(left, right, preferred_element_type=F32)


def on_core(core):
    return lax.axis_index("depth") % 2 == core


def on_chip(chip):
    return lax.axis_index("depth") // 2 == chip


def group_of(hop):
    part, at = divmod(hop, len(GROUPS[0]))
    return GROUPS[part % len(GROUPS)][at]


def tiles(width, tile, body, unroll):
    if unroll:
        for at in range(0, width, tile):
            body(pl.ds(at, tile))
    else:
        pl.loop(0, width // tile)(lambda i: body(pl.ds(pl.multiple_of(i * tile, tile), tile)))


def halves(value):
    high = value.astype(BF)
    return high, (value - high.astype(F32)).astype(BF)


def split_dot(left, right):
    rows = left.shape[0]
    both = dot(jnp.concatenate(halves(left), 0), right)
    return both[:rows] + both[rows:]


def in_vmem(*arrays):
    return tuple(pltpu.with_memory_space_constraint(a, pltpu.VMEM) for a in arrays)


def call(kernel, outs, specs, flops, limit=8, scratch=(), out_specs=None, aliases=None):
    return pl.pallas_call(
        kernel,
        out_shape=outs,
        in_specs=specs,
        out_specs=out_specs or jax.tree.map(lambda _: IN_VMEM, outs),
        scratch_shapes=scratch,
        input_output_aliases=aliases or {},
        compiler_params=pltpu.CompilerParams(vmem_limit_bytes=limit << 20),
        cost_estimate=pl.CostEstimate(flops=flops, bytes_accessed=1 << 20, transcendentals=0),
    )


def layer(state, query, key, value, out_map, waits, normed, context, result):
    rows = state[...]
    centred = rows - jnp.mean(rows, axis=-1, keepdims=True)
    row_var = jnp.mean(centred * centred, axis=-1, keepdims=True)
    normed[...] = (centred * lax.rsqrt(row_var + 1e-05)).astype(BF)
    for wait in waits[:3]:
        wait()

    def project_in(at):
        n, cols = normed[...], slice(at, at + TILE)
        return tuple(dot(n, w[:, cols]).astype(BF) for w in (query, key, value))

    ahead = project_in(0)
    for at in range(0, INNER, TILE):
        q, k, v = ahead
        ones = [slice(one, one + HEAD_DIM) for one in range(0, TILE, HEAD_DIM)]
        scores = [
            lax.dot_general(q[:, one], k[:, one], (((1,), (1,)), ((), ())), preferred_element_type=F32)
            for one in ones
        ]
        if at + TILE < INNER:
            ahead = project_in(at + TILE)
        for one, score in zip(ones, scores):
            grown = jnp.exp2((score - jnp.max(score, axis=-1, keepdims=True)) * EXPONENT)
            share = 1.0 / jnp.sum(grown, axis=-1, keepdims=True)
            context[:, at + one.start : at + one.stop] = dot((grown * share).astype(BF), v[:, one]).astype(BF)

    waits[3]()

    def project(cols):
        result[:, cols] = state[:, cols] + dot(context[...], out_map[:, cols])

    tiles(state.shape[1], TILE, project, UNROLL)


def load_kernel(c, here, sem):
    move = pltpu.make_async_copy(c.at[0], here, sem.at[0])
    move.start()
    move.wait()


def maps_kernel(w_query, w_key, w_value, w_out, own, own_high, query, key, value, v1, o1, sems):
    moves = [
        pltpu.make_async_copy(src.at[at], dst, sems.at[i])
        for i, (src, at, dst) in enumerate(
            [(w_value, 1, v1), (w_out, 1, o1), (w_query, 0, query), (w_key, 0, key), (w_value, 0, value)]
        )
    ]
    for move in moves:
        move.start()
    moves[0].wait()
    moves[1].wait()

    @pl.loop(0, own.shape[0] // 256)
    def _(block):
        rows = pl.ds(pl.multiple_of(block * 256, 256), 256)
        product = 0.25 * dot(v1[rows, :], o1[...])
        own[rows, :] = product
        own_high[rows, :] = product.astype(BF)

    for move in moves[2:]:
        move.wait()


def advance_kernel(
    c, query, key, value, w_query, w_key, w_value, w_out, out, o0, q1, k1, v1, o1, middle, normed, context, sems
):
    moves = [
        pltpu.make_async_copy(src.at[at], dst, sems.at[i])
        for i, (src, at, dst) in enumerate(
            [(w_out, 0, o0), (w_query, 1, q1), (w_key, 1, k1), (w_value, 1, v1), (w_out, 1, o1)]
        )
    ]
    for move in moves:
        move.start()
    here = lambda: None
    layer(c, query, key, value, o0, [here, here, here, moves[0].wait], normed, context, middle)
    layer(middle, q1, k1, v1, o1, [move.wait for move in moves[1:]], normed, context, out)


def subtract_kernel(left, right, out):
    out[...] = left[...] - right[...]


def cast_kernel(wide, out):
    @pl.loop(0, wide.shape[0] // 128)
    def _(block):
        rows = pl.ds(pl.multiple_of(block * 128, 128), 128)
        out[rows, :] = wide[rows, :].astype(BF)


def add_kernel(left, right, out):
    out[...] = left[...] + right[...]


def product_kernel(own, other, own_high, other_high, c_high, c_low):
    def body(first, second):
        @pl.loop(0, own.shape[0] // 256)
        def _(block):
            rows = pl.ds(pl.multiple_of(block * 256, 256), 256)
            for at in range(0, own.shape[1], 256):
                cols = slice(at, at + 256)
                total = dot(first[rows, :], second[:, cols]) + (own[rows, cols] + other[rows, cols])
                c_high[rows, cols], c_low[rows, cols] = halves(total)

    here = jnp.logical_not(on_chip(0))
    pl.when(here & on_core(0))(lambda: body(own_high, other_high))
    pl.when(here & on_core(1))(lambda: body(other_high, own_high))


def source_kernel(mine, theirs, own_high, other_high, r0_half, *out):
    half = r0_half.shape[0]
    rows = half // CHUNKS

    def body(r0, r1, at, high):
        r0_half[...] = r0[at : at + half, :]
        total = r1[at : at + half, :] + r0[at : at + half, :] + split_dot(r0[at : at + half, :], high[...])
        for j in range(CHUNKS):
            out[j][...] = total[j * rows : (j + 1) * rows]

    pl.when(on_core(0))(lambda: body(mine, theirs, 0, other_high))
    pl.when(on_core(1))(lambda: body(theirs, mine, half, own_high))


def squares_kernel(mine, theirs, out):
    def tile(ref):
        def body(at, total):
            rows = ref[pl.ds(pl.multiple_of(at * 8, 8), 8), :]
            return total + rows * rows

        total = lax.fori_loop(0, ref.shape[0] // 8, body, jnp.zeros((8, ref.shape[1]), F32))
        return sum(total[:, at : at + 128] for at in range(0, ref.shape[1], 128))

    last = lax.axis_size("depth") - 1
    me = lax.axis_index("depth")
    zero = jnp.zeros(out.shape, F32)
    a = jnp.where(me != last, tile(mine), zero)
    out[...] = a + jnp.where(me != last - 1, tile(theirs), zero)


def times_chunk(e, matrix, body, low=None):
    rows = e.shape[0]
    e_high, e_low = halves(e)
    both = jnp.concatenate([e_high, e_low], 0)

    def part(cols):
        wide = dot(both, matrix[:, cols])
        product = wide[:rows] + wide[rows:]
        body(cols, product if low is None else product + dot(e_high, low[:, cols]))

    tiles(matrix.shape[1], HOP_TILE, part, True)


def hop_kernel(hop, received, *refs):
    source, c_high, c_low, sent, kept = refs[-5:]

    @pl.when(on_chip(hop + 1))
    def _():
        kept[...] = received[...]

        def body(cols, product):
            sent[:, cols] = received[:, cols] + source[:, cols] + product

        times_chunk(received[...], c_high, body, c_low)

    @pl.when(jnp.logical_not(on_chip(hop + 1)))
    def _():
        kept[...] = jnp.zeros_like(kept) if hop == 0 else refs[0][...]


def last_kernel(chunk, hop, received, before, r0_half, own_high, other_high, mine, sent):
    rows = received.shape[0]

    def body(kept, first, second, high):
        first[...] = kept

        def part(cols, product):
            second[:, cols] = (
                first[:, cols] + product + r0_half[chunk * rows : (chunk + 1) * rows, cols]
            )

        times_chunk(kept, high, part)

    e = jnp.where(on_chip(hop + 1), received[...], before[...])
    pl.when(on_core(0))(lambda: body(e, mine, sent, own_high))
    pl.when(on_core(1))(lambda: body(e, sent, mine, other_high))


def finish_kernel(count, *refs):
    mine, theirs = refs[:CHUNKS], refs[CHUNKS : 2 * CHUNKS]
    own_high, w, c, total, q0, k0, v0, o0, out, rms = refs[2 * CHUNKS : 2 * CHUNKS + 10]
    x, u, result, normed, context, sems = refs[2 * CHUNKS + 10 :]
    rows = mine[0].shape[0]
    half = rows * CHUNKS

    def gather(low, high):
        for j in range(CHUNKS):
            x[j * rows : (j + 1) * rows, :] = low[j][...]
            x[half + j * rows : half + (j + 1) * rows, :] = high[j][...]

    pl.when(on_core(0))(lambda: gather(mine, theirs))
    pl.when(on_core(1))(lambda: gather(theirs, mine))
    u[...] = c[...] + x[...]

    def carry(cols, product):
        result[1, :, cols] = w[:, cols] + x[:, cols] + product

    times_chunk(x[...], own_high, carry)
    mean_sq = jnp.sum(total[...], keepdims=True) / count
    rms[0] = jnp.sqrt(mean_sq)[0, 0]
    second = pltpu.make_async_copy(result.at[1], out.at[1], sems.at[0])
    second.start()
    layer(u, q0, k0, v0, o0, [lambda: None] * 4, normed, context, result.at[0])
    first = pltpu.make_async_copy(result.at[0], out.at[0], sems.at[1])
    first.start()
    first.wait()
    second.wait()


def per_device(c_states, w_query, w_key, w_value, w_out):
    dev_count = lax.axis_size("depth")
    chips = dev_count // 2
    tokens, width = c_states.shape[1:]
    half = tokens // 2
    rows = half // CHUNKS
    swap_pairs = [(i, i ^ 1) for i in range(dev_count)]
    dma = pltpu.SemaphoreType.DMA

    def swap(block):
        return lax.ppermute(block, "depth", swap_pairs)

    def f32_of(*shape):
        return pltpu.VMEM(shape, F32)

    def bf_of(*shape):
        return pltpu.VMEM(shape, BF)

    square = bf_of(width, width)
    state = f32_of(tokens, width)
    chunk = f32_of(rows, width)
    thin = bf_of(tokens, width)

    c_states, w_query, w_key, w_value, w_out = (
        pltpu.with_memory_space_constraint(w, pltpu.HBM) for w in (c_states, w_query, w_key, w_value, w_out)
    )
    c_guess = call(load_kernel, state, [IN_PLACE], 1, limit=4, scratch=[dma((1,))])(c_states)
    next_state = lax.ppermute(c_guess, "depth", [(i, i - 1) for i in range(1, dev_count)])
    own, own_high, query, key, value = call(
        maps_kernel,
        (f32_of(width, width),) + (square,) * 4,
        [IN_PLACE] * 4,
        1 << 20,
        limit=16,
        scratch=[square, square, dma((5,))],
    )(w_query, w_key, w_value, w_out)
    other = swap(own)
    query, key, value, c_guess = in_vmem(query, key, value, c_guess)
    fine_c, out_map = call(
        advance_kernel,
        (state, square),
        [IN_VMEM] * 4 + [IN_PLACE] * 4,
        1 << 20,
        limit=28,
        scratch=[square] * 4 + [state, thin, thin, dma((5,))],
    )(c_guess, query, key, value, w_query, w_key, w_value, w_out)
    fine_c, next_state = in_vmem(fine_c, next_state)
    residual = call(subtract_kernel, state, [IN_VMEM] * 2, 1 << 35, limit=4)(fine_c, next_state)
    other_residual = swap(residual)
    own, other, own_high = in_vmem(own, other, own_high)
    other_high, residual = in_vmem(
        call(cast_kernel, square, [IN_VMEM], 1 << 20, limit=4)(other), residual
    )
    c_high, c_low = call(product_kernel, (square, square), [IN_VMEM] * 4, 2 * width**3, limit=16)(
        own, other, own_high, other_high
    )
    other_residual, c_high = lax.optimization_barrier((other_residual, c_high))
    other_residual, c_high, c_low = in_vmem(other_residual, c_high, c_low)
    r0_half, *source = call(
        source_kernel,
        (f32_of(half, width),) + (chunk,) * CHUNKS,
        [IN_VMEM] * 4,
        4 * half * width * width,
    )(residual, other_residual, own_high, other_high)
    sent = list(source)
    source = in_vmem(*source)
    kept = [None] * CHUNKS
    for hop in range(chips - 1):
        if hop == 3:
            residual, sent[-1] = lax.optimization_barrier((residual, sent[-1]))
            (residual,) = in_vmem(residual)
            total = call(squares_kernel, f32_of(8, 128), [IN_VMEM] * 2, 1 << 20, limit=4)(
                residual, other_residual
            )
        if hop in ROUNDS:
            reach = ROUNDS[hop]
            total, sent[-1] = lax.optimization_barrier((total, sent[-1]))
            theirs = lax.ppermute(total, "depth", [(i, i ^ reach) for i in range(dev_count)])
            total = call(add_kernel, f32_of(8, 128), [IN_VMEM] * 2, 1 << 12, limit=4)(total, theirs)
            kept[0], total = lax.optimization_barrier((kept[0], total))
        alike = [at for at in range(chips - 1) if group_of(at) == group_of(hop)]
        pairs = [(2 * at + i, 2 * at + 2 + i) for at in alike for i in range(2)]
        for j in range(CHUNKS):
            received = lax.ppermute(sent[j], "depth", pairs)
            held = in_vmem(received) if hop == 0 else in_vmem(received, kept[j])
            if hop < chips - 2:
                sent[j], kept[j] = call(
                    functools.partial(hop_kernel, hop),
                    (chunk, chunk),
                    [IN_VMEM] * (len(held) + 3),
                    4 * rows * width * width,
                    limit=4,
                )(*held, source[j], c_high, c_low)
            else:
                kept[j], sent[j] = call(
                    functools.partial(last_kernel, j, hop),
                    (chunk, chunk),
                    [IN_VMEM] * 5,
                    4 * rows * width * width,
                    limit=4,
                )(*held, r0_half, own_high, other_high)
    crossed = in_vmem(*[swap(block) for block in sent])
    kept = in_vmem(*kept)
    (out_map,) = in_vmem(out_map)
    return call(
        functools.partial(finish_kernel, float((dev_count - 1) * tokens * width)),
        (jax.ShapeDtypeStruct((2, tokens, width), F32), jax.ShapeDtypeStruct((1,), F32)),
        [IN_VMEM] * (2 * CHUNKS + 8),
        18 * tokens * width * width,
        limit=20,
        scratch=[state, state, f32_of(2, tokens, width), thin, thin, dma((2,))],
        out_specs=(IN_PLACE, IN_SMEM),
    )(*kept, *crossed, own_high, fine_c, c_guess, total, query, key, value, out_map)


def solution(mesh):
    in_specs = (
        P("depth", "dp", None),
        P("depth", None, None),
        P("depth", None, None),
        P("depth", None, None),
        P("depth", None, None),
    )
    out_specs = (P("depth", "dp", None), P("dp"))
    return jax.shard_map(
        per_device, mesh=mesh, in_specs=in_specs, out_specs=out_specs, check_vma=False
    )
```

```python
import functools

import jax
import jax.numpy as jnp
from jax import lax
from jax.experimental import pallas as pl
from jax.experimental.pallas import tpu as pltpu
from jax.sharding import PartitionSpec as P

HEADS = 8
HEAD_DIM = 128
INNER = 1024
CHUNKS = 4
EXPONENT = HEAD_DIM ** (-0.5) * 1.4426950408889634
GROUPS = ((0, 1, 2, 3, 4), (0, 3, 1, 4, 2), (1, 2, 0, 4, 3))
ROUNDS = {4: 16, 9: 8, 11: 4, 13: 2}
TILE = 256
UNROLL = True
HOP_TILE = 256

BF = jnp.bfloat16
F32 = jnp.float32
IN_VMEM = pl.BlockSpec(memory_space=pltpu.VMEM)
IN_SMEM = pl.BlockSpec(memory_space=pltpu.SMEM)
IN_PLACE = pl.BlockSpec(memory_space=pltpu.HBM)


def dot(left, right):
    return jnp.dot(left, right, preferred_element_type=F32)


def on_core(core):
    return lax.axis_index("depth") % 2 == core


def on_chip(chip):
    return lax.axis_index("depth") // 2 == chip


def group_of(hop):
    part, at = divmod(hop, len(GROUPS[0]))
    return GROUPS[part % len(GROUPS)][at]


def tiles(width, tile, body, unroll):
    if unroll:
        for at in range(0, width, tile):
            body(pl.ds(at, tile))
    else:
        pl.loop(0, width // tile)(lambda i: body(pl.ds(pl.multiple_of(i * tile, tile), tile)))


def halves(value):
    high = value.astype(BF)
    return high, (value - high.astype(F32)).astype(BF)


def split_dot(left, right):
    rows = left.shape[0]
    both = dot(jnp.concatenate(halves(left), 0), right)
    return both[:rows] + both[rows:]


def in_vmem(*arrays):
    return tuple(pltpu.with_memory_space_constraint(a, pltpu.VMEM) for a in arrays)


def call(kernel, outs, specs, flops, limit=8, scratch=(), out_specs=None, aliases=None):
    return pl.pallas_call(
        kernel,
        out_shape=outs,
        in_specs=specs,
        out_specs=out_specs or jax.tree.map(lambda _: IN_VMEM, outs),
        scratch_shapes=scratch,
        input_output_aliases=aliases or {},
        compiler_params=pltpu.CompilerParams(vmem_limit_bytes=limit << 20),
        cost_estimate=pl.CostEstimate(flops=flops, bytes_accessed=1 << 20, transcendentals=0),
    )


def layer(state, query, key, value, out_map, waits, normed, context, result):
    rows = state[...]
    centred = rows - jnp.mean(rows, axis=-1, keepdims=True)
    row_var = jnp.mean(centred * centred, axis=-1, keepdims=True)
    normed[...] = (centred * lax.rsqrt(row_var + 1e-05)).astype(BF)
    for wait in waits[:3]:
        wait()

    def project_in(at):
        n, cols = normed[...], slice(at, at + TILE)
        return tuple(dot(n, w[:, cols]).astype(BF) for w in (query, key, value))

    ahead = project_in(0)
    for at in range(0, INNER, TILE):
        q, k, v = ahead
        ones = [slice(one, one + HEAD_DIM) for one in range(0, TILE, HEAD_DIM)]
        scores = [
            lax.dot_general(q[:, one], k[:, one], (((1,), (1,)), ((), ())), preferred_element_type=F32)
            for one in ones
        ]
        if at + TILE < INNER:
            ahead = project_in(at + TILE)
        for one, score in zip(ones, scores):
            grown = jnp.exp2((score - jnp.max(score, axis=-1, keepdims=True)) * EXPONENT)
            share = 1.0 / jnp.sum(grown, axis=-1, keepdims=True)
            context[:, at + one.start : at + one.stop] = dot((grown * share).astype(BF), v[:, one]).astype(BF)

    waits[3]()

    def project(cols):
        result[:, cols] = state[:, cols] + dot(context[...], out_map[:, cols])

    tiles(state.shape[1], TILE, project, UNROLL)


def maps_kernel(w_query, w_key, w_value, w_out, c, own, own_high, query, key, value, c_here, v1, o1, sems):
    moves = [
        pltpu.make_async_copy(src.at[at], dst, sems.at[i])
        for i, (src, at, dst) in enumerate(
            [(w_value, 1, v1), (w_out, 1, o1), (w_query, 0, query), (w_key, 0, key), (w_value, 0, value)]
        )
    ]
    moves.append(pltpu.make_async_copy(c.at[0], c_here, sems.at[5]))
    for move in moves:
        move.start()
    moves[0].wait()
    moves[1].wait()

    @pl.loop(0, own.shape[0] // 256)
    def _(block):
        rows = pl.ds(pl.multiple_of(block * 256, 256), 256)
        product = 0.25 * dot(v1[rows, :], o1[...])
        own[rows, :] = product
        own_high[rows, :] = product.astype(BF)

    for move in moves[2:]:
        move.wait()


def advance_kernel(
    c, query, key, value, w_query, w_key, w_value, w_out, out, o0, q1, k1, v1, o1, middle, normed, context, sems
):
    moves = [
        pltpu.make_async_copy(src.at[at], dst, sems.at[i])
        for i, (src, at, dst) in enumerate(
            [(w_out, 0, o0), (w_query, 1, q1), (w_key, 1, k1), (w_value, 1, v1), (w_out, 1, o1)]
        )
    ]
    for move in moves:
        move.start()
    here = lambda: None
    layer(c, query, key, value, o0, [here, here, here, moves[0].wait], normed, context, middle)
    layer(middle, q1, k1, v1, o1, [move.wait for move in moves[1:]], normed, context, out)


def subtract_kernel(left, right, out):
    out[...] = left[...] - right[...]


def cast_kernel(wide, out):
    @pl.loop(0, wide.shape[0] // 128)
    def _(block):
        rows = pl.ds(pl.multiple_of(block * 128, 128), 128)
        out[rows, :] = wide[rows, :].astype(BF)


def add_kernel(left, right, out):
    out[...] = left[...] + right[...]


def product_kernel(own, other, own_high, other_high, c_high, c_low):
    def body(first, second):
        @pl.loop(0, own.shape[0] // 256)
        def _(block):
            rows = pl.ds(pl.multiple_of(block * 256, 256), 256)
            for at in range(0, own.shape[1], 256):
                cols = slice(at, at + 256)
                total = dot(first[rows, :], second[:, cols]) + (own[rows, cols] + other[rows, cols])
                c_high[rows, cols], c_low[rows, cols] = halves(total)

    here = jnp.logical_not(on_chip(0))
    pl.when(here & on_core(0))(lambda: body(own_high, other_high))
    pl.when(here & on_core(1))(lambda: body(other_high, own_high))


def source_kernel(mine, theirs, own_high, other_high, r0_half, *out):
    half = r0_half.shape[0]
    rows = half // CHUNKS

    def body(r0, r1, at, high):
        r0_half[...] = r0[at : at + half, :]
        total = r1[at : at + half, :] + r0[at : at + half, :] + split_dot(r0[at : at + half, :], high[...])
        for j in range(CHUNKS):
            out[j][...] = total[j * rows : (j + 1) * rows]

    pl.when(on_core(0))(lambda: body(mine, theirs, 0, other_high))
    pl.when(on_core(1))(lambda: body(theirs, mine, half, own_high))


def squares_kernel(mine, theirs, out):
    def tile(ref):
        def body(at, total):
            rows = ref[pl.ds(pl.multiple_of(at * 8, 8), 8), :]
            return total + rows * rows

        total = lax.fori_loop(0, ref.shape[0] // 8, body, jnp.zeros((8, ref.shape[1]), F32))
        return sum(total[:, at : at + 128] for at in range(0, ref.shape[1], 128))

    last = lax.axis_size("depth") - 1
    me = lax.axis_index("depth")
    zero = jnp.zeros(out.shape, F32)
    a = jnp.where(me != last, tile(mine), zero)
    out[...] = a + jnp.where(me != last - 1, tile(theirs), zero)


def times_chunk(e, matrix, body, low=None):
    rows = e.shape[0]
    e_high, e_low = halves(e)
    both = jnp.concatenate([e_high, e_low], 0)

    def part(cols):
        wide = dot(both, matrix[:, cols])
        product = wide[:rows] + wide[rows:]
        body(cols, product if low is None else product + dot(e_high, low[:, cols]))

    tiles(matrix.shape[1], HOP_TILE, part, True)


def hop_kernel(hop, received, *refs):
    source, c_high, c_low, sent, kept = refs[-5:]

    @pl.when(on_chip(hop + 1))
    def _():
        kept[...] = received[...]

        def body(cols, product):
            sent[:, cols] = received[:, cols] + source[:, cols] + product

        times_chunk(received[...], c_high, body, c_low)

    @pl.when(jnp.logical_not(on_chip(hop + 1)))
    def _():
        kept[...] = jnp.zeros_like(kept) if hop == 0 else refs[0][...]


def last_kernel(chunk, hop, received, before, r0_half, own_high, other_high, mine, sent):
    rows = received.shape[0]

    def body(kept, first, second, high):
        first[...] = kept

        def part(cols, product):
            second[:, cols] = (
                first[:, cols] + product + r0_half[chunk * rows : (chunk + 1) * rows, cols]
            )

        times_chunk(kept, high, part)

    e = jnp.where(on_chip(hop + 1), received[...], before[...])
    pl.when(on_core(0))(lambda: body(e, mine, sent, own_high))
    pl.when(on_core(1))(lambda: body(e, sent, mine, other_high))


def finish_kernel(count, *refs):
    mine, theirs = refs[:CHUNKS], refs[CHUNKS : 2 * CHUNKS]
    own_high, w, c, total, q0, k0, v0, o0, out, rms = refs[2 * CHUNKS : 2 * CHUNKS + 10]
    x, u, result, normed, context, sems = refs[2 * CHUNKS + 10 :]
    rows = mine[0].shape[0]
    half = rows * CHUNKS

    def gather(low, high):
        for j in range(CHUNKS):
            x[j * rows : (j + 1) * rows, :] = low[j][...]
            x[half + j * rows : half + (j + 1) * rows, :] = high[j][...]

    pl.when(on_core(0))(lambda: gather(mine, theirs))
    pl.when(on_core(1))(lambda: gather(theirs, mine))
    u[...] = c[...] + x[...]

    def carry(cols, product):
        result[1, :, cols] = w[:, cols] + x[:, cols] + product

    times_chunk(x[...], own_high, carry)
    mean_sq = jnp.sum(total[...], keepdims=True) / count
    rms[0] = jnp.sqrt(mean_sq)[0, 0]
    second = pltpu.make_async_copy(result.at[1], out.at[1], sems.at[0])
    second.start()
    layer(u, q0, k0, v0, o0, [lambda: None] * 4, normed, context, result.at[0])
    first = pltpu.make_async_copy(result.at[0], out.at[0], sems.at[1])
    first.start()
    first.wait()
    second.wait()


def per_device(c_states, w_query, w_key, w_value, w_out):
    dev_count = lax.axis_size("depth")
    chips = dev_count // 2
    tokens, width = c_states.shape[1:]
    half = tokens // 2
    rows = half // CHUNKS
    swap_pairs = [(i, i ^ 1) for i in range(dev_count)]
    dma = pltpu.SemaphoreType.DMA

    def swap(block):
        return lax.ppermute(block, "depth", swap_pairs)

    def f32_of(*shape):
        return pltpu.VMEM(shape, F32)

    def bf_of(*shape):
        return pltpu.VMEM(shape, BF)

    square = bf_of(width, width)
    state = f32_of(tokens, width)
    chunk = f32_of(rows, width)
    thin = bf_of(tokens, width)

    guess = c_states[0]
    c_states, w_query, w_key, w_value, w_out = (
        pltpu.with_memory_space_constraint(w, pltpu.HBM) for w in (c_states, w_query, w_key, w_value, w_out)
    )
    next_state = lax.ppermute(guess, "depth", [(i, i - 1) for i in range(1, dev_count)])
    own, own_high, query, key, value, c_guess = call(
        maps_kernel,
        (f32_of(width, width),) + (square,) * 4 + (state,),
        [IN_PLACE] * 5,
        1 << 20,
        limit=16,
        scratch=[square, square, dma((6,))],
    )(w_query, w_key, w_value, w_out, c_states)
    other = swap(own)
    query, key, value, c_guess = in_vmem(query, key, value, c_guess)
    fine_c, out_map = call(
        advance_kernel,
        (state, square),
        [IN_VMEM] * 4 + [IN_PLACE] * 4,
        1 << 20,
        limit=28,
        scratch=[square] * 4 + [state, thin, thin, dma((5,))],
    )(c_guess, query, key, value, w_query, w_key, w_value, w_out)
    fine_c, next_state = in_vmem(fine_c, next_state)
    residual = call(subtract_kernel, state, [IN_VMEM] * 2, 1 << 35, limit=4)(fine_c, next_state)
    other_residual = swap(residual)
    own, other, own_high = in_vmem(own, other, own_high)
    other_high, residual = in_vmem(
        call(cast_kernel, square, [IN_VMEM], 1 << 20, limit=4)(other), residual
    )
    c_high, c_low = call(product_kernel, (square, square), [IN_VMEM] * 4, 2 * width**3, limit=16)(
        own, other, own_high, other_high
    )
    other_residual, c_high = lax.optimization_barrier((other_residual, c_high))
    other_residual, c_high, c_low = in_vmem(other_residual, c_high, c_low)
    r0_half, *source = call(
        source_kernel,
        (f32_of(half, width),) + (chunk,) * CHUNKS,
        [IN_VMEM] * 4,
        4 * half * width * width,
    )(residual, other_residual, own_high, other_high)
    sent = list(source)
    source = in_vmem(*source)
    kept = [None] * CHUNKS
    for hop in range(chips - 1):
        if hop == 3:
            residual, sent[-1] = lax.optimization_barrier((residual, sent[-1]))
            (residual,) = in_vmem(residual)
            total = call(squares_kernel, f32_of(8, 128), [IN_VMEM] * 2, 1 << 20, limit=4)(
                residual, other_residual
            )
        if hop in ROUNDS:
            reach = ROUNDS[hop]
            total, sent[-1] = lax.optimization_barrier((total, sent[-1]))
            theirs = lax.ppermute(total, "depth", [(i, i ^ reach) for i in range(dev_count)])
            total = call(add_kernel, f32_of(8, 128), [IN_VMEM] * 2, 1 << 12, limit=4)(total, theirs)
            kept[0], total = lax.optimization_barrier((kept[0], total))
        alike = [at for at in range(chips - 1) if group_of(at) == group_of(hop)]
        pairs = [(2 * at + i, 2 * at + 2 + i) for at in alike for i in range(2)]
        for j in range(CHUNKS):
            received = lax.ppermute(sent[j], "depth", pairs)
            held = in_vmem(received) if hop == 0 else in_vmem(received, kept[j])
            if hop < chips - 2:
                sent[j], kept[j] = call(
                    functools.partial(hop_kernel, hop),
                    (chunk, chunk),
                    [IN_VMEM] * (len(held) + 3),
                    4 * rows * width * width,
                    limit=4,
                )(*held, source[j], c_high, c_low)
            else:
                kept[j], sent[j] = call(
                    functools.partial(last_kernel, j, hop),
                    (chunk, chunk),
                    [IN_VMEM] * 5,
                    4 * rows * width * width,
                    limit=4,
                )(*held, r0_half, own_high, other_high)
    crossed = in_vmem(*[swap(block) for block in sent])
    kept = in_vmem(*kept)
    (out_map,) = in_vmem(out_map)
    return call(
        functools.partial(finish_kernel, float((dev_count - 1) * tokens * width)),
        (jax.ShapeDtypeStruct((2, tokens, width), F32), jax.ShapeDtypeStruct((1,), F32)),
        [IN_VMEM] * (2 * CHUNKS + 8),
        18 * tokens * width * width,
        limit=20,
        scratch=[state, state, f32_of(2, tokens, width), thin, thin, dma((2,))],
        out_specs=(IN_PLACE, IN_SMEM),
    )(*kept, *crossed, own_high, fine_c, c_guess, total, query, key, value, out_map)


def solution(mesh):
    in_specs = (
        P("depth", "dp", None),
        P("depth", None, None),
        P("depth", None, None),
        P("depth", None, None),
        P("depth", None, None),
    )
    out_specs = (P("depth", "dp", None), P("dp"))
    return jax.shard_map(
        per_device, mesh=mesh, in_specs=in_specs, out_specs=out_specs, check_vma=False
    )
```

```python
import functools

import jax
import jax.numpy as jnp
from jax import lax
from jax.experimental import pallas as pl
from jax.experimental.pallas import tpu as pltpu
from jax.sharding import PartitionSpec as P

HEADS = 8
HEAD_DIM = 128
INNER = 1024
CHUNKS = 4
EXPONENT = HEAD_DIM ** (-0.5) * 1.4426950408889634
GROUPS = ((0, 1, 2, 3, 4), (0, 3, 1, 4, 2), (1, 2, 0, 4, 3))
ROUNDS = {4: 16, 9: 8, 11: 4, 13: 2}
TILE = 256
UNROLL = True
HOP_TILE = 256

BF = jnp.bfloat16
F32 = jnp.float32
IN_VMEM = pl.BlockSpec(memory_space=pltpu.VMEM)
IN_SMEM = pl.BlockSpec(memory_space=pltpu.SMEM)
IN_PLACE = pl.BlockSpec(memory_space=pltpu.HBM)


def dot(left, right):
    return jnp.dot(left, right, preferred_element_type=F32)


def on_core(core):
    return lax.axis_index("depth") % 2 == core


def on_chip(chip):
    return lax.axis_index("depth") // 2 == chip


def group_of(hop):
    part, at = divmod(hop, len(GROUPS[0]))
    return GROUPS[part % len(GROUPS)][at]


def tiles(width, tile, body, unroll):
    if unroll:
        for at in range(0, width, tile):
            body(pl.ds(at, tile))
    else:
        pl.loop(0, width // tile)(lambda i: body(pl.ds(pl.multiple_of(i * tile, tile), tile)))


def halves(value):
    high = value.astype(BF)
    return high, (value - high.astype(F32)).astype(BF)


def split_dot(left, right):
    rows = left.shape[0]
    both = dot(jnp.concatenate(halves(left), 0), right)
    return both[:rows] + both[rows:]


def in_vmem(*arrays):
    return tuple(pltpu.with_memory_space_constraint(a, pltpu.VMEM) for a in arrays)


def call(kernel, outs, specs, flops, limit=8, scratch=(), out_specs=None, aliases=None):
    return pl.pallas_call(
        kernel,
        out_shape=outs,
        in_specs=specs,
        out_specs=out_specs or jax.tree.map(lambda _: IN_VMEM, outs),
        scratch_shapes=scratch,
        input_output_aliases=aliases or {},
        compiler_params=pltpu.CompilerParams(vmem_limit_bytes=limit << 20),
        cost_estimate=pl.CostEstimate(flops=flops, bytes_accessed=1 << 20, transcendentals=0),
    )


def layer(state, query, key, value, out_map, waits, normed, context, result):
    rows = state[...]
    centred = rows - jnp.mean(rows, axis=-1, keepdims=True)
    row_var = jnp.mean(centred * centred, axis=-1, keepdims=True)
    normed[...] = (centred * lax.rsqrt(row_var + 1e-05)).astype(BF)
    for wait in waits[:3]:
        wait()

    def project_in(at):
        n, cols = normed[...], slice(at, at + TILE)
        return tuple(dot(n, w[:, cols]).astype(BF) for w in (query, key, value))

    ahead = project_in(0)
    for at in range(0, INNER, TILE):
        q, k, v = ahead
        ones = [slice(one, one + HEAD_DIM) for one in range(0, TILE, HEAD_DIM)]
        scores = [
            lax.dot_general(q[:, one], k[:, one], (((1,), (1,)), ((), ())), preferred_element_type=F32)
            for one in ones
        ]
        if at + TILE < INNER:
            ahead = project_in(at + TILE)
        for one, score in zip(ones, scores):
            grown = jnp.exp2((score - jnp.max(score, axis=-1, keepdims=True)) * EXPONENT)
            share = 1.0 / jnp.sum(grown, axis=-1, keepdims=True)
            context[:, at + one.start : at + one.stop] = dot((grown * share).astype(BF), v[:, one]).astype(BF)

    waits[3]()

    def project(cols):
        result[:, cols] = state[:, cols] + dot(context[...], out_map[:, cols])

    tiles(state.shape[1], TILE, project, UNROLL)


def maps_kernel(w_query, w_key, w_value, w_out, c, own, own_high, query, key, value, c_here, v1, o1, sems):
    moves = [
        pltpu.make_async_copy(src.at[at], dst, sems.at[i])
        for i, (src, at, dst) in enumerate(
            [(w_value, 1, v1), (w_out, 1, o1), (w_query, 0, query), (w_key, 0, key), (w_value, 0, value)]
        )
    ]
    moves.append(pltpu.make_async_copy(c.at[0], c_here, sems.at[5]))
    for move in moves:
        move.start()
    moves[0].wait()
    moves[1].wait()

    @pl.loop(0, own.shape[0] // 256)
    def _(block):
        rows = pl.ds(pl.multiple_of(block * 256, 256), 256)
        product = 0.25 * dot(v1[rows, :], o1[...])
        own[rows, :] = product
        own_high[rows, :] = product.astype(BF)

    for move in moves[2:]:
        move.wait()


def advance_kernel(
    c, query, key, value, w_query, w_key, w_value, w_out, out, o0, q1, k1, v1, o1, middle, normed, context, sems
):
    moves = [
        pltpu.make_async_copy(src.at[at], dst, sems.at[i])
        for i, (src, at, dst) in enumerate(
            [(w_out, 0, o0), (w_query, 1, q1), (w_key, 1, k1), (w_value, 1, v1), (w_out, 1, o1)]
        )
    ]
    for move in moves:
        move.start()
    here = lambda: None
    layer(c, query, key, value, o0, [here, here, here, moves[0].wait], normed, context, middle)
    layer(middle, q1, k1, v1, o1, [move.wait for move in moves[1:]], normed, context, out)


def subtract_kernel(left, right, out):
    out[...] = left[...] - right[...]


def cast_kernel(wide, out):
    @pl.loop(0, wide.shape[0] // 128)
    def _(block):
        rows = pl.ds(pl.multiple_of(block * 128, 128), 128)
        out[rows, :] = wide[rows, :].astype(BF)


def add_kernel(left, right, out):
    out[...] = left[...] + right[...]


def product_kernel(late, own, other, own_high, other_high, *refs):
    c_high, c_low = refs[-2:]

    def body(first, second):
        @pl.loop(0, own.shape[0] // 256)
        def _(block):
            rows = pl.ds(pl.multiple_of(block * 256, 256), 256)
            for at in range(0, own.shape[1], 256):
                cols = slice(at, at + 256)
                total = dot(first[rows, :], second[:, cols]) + (own[rows, cols] + other[rows, cols])
                c_high[rows, cols], c_low[rows, cols] = halves(total)

    here = on_chip(1) if late else jnp.logical_not(on_chip(0) | on_chip(1))
    pl.when(here & on_core(0))(lambda: body(own_high, other_high))
    pl.when(here & on_core(1))(lambda: body(other_high, own_high))


def source_kernel(mine, theirs, own_high, other_high, r0_half, *out):
    half = r0_half.shape[0]
    rows = half // CHUNKS

    def body(r0, r1, at, high):
        r0_half[...] = r0[at : at + half, :]
        total = r1[at : at + half, :] + r0[at : at + half, :] + split_dot(r0[at : at + half, :], high[...])
        for j in range(CHUNKS):
            out[j][...] = total[j * rows : (j + 1) * rows]

    pl.when(on_core(0))(lambda: body(mine, theirs, 0, other_high))
    pl.when(on_core(1))(lambda: body(theirs, mine, half, own_high))


def squares_kernel(mine, theirs, out):
    def tile(ref):
        def body(at, total):
            rows = ref[pl.ds(pl.multiple_of(at * 8, 8), 8), :]
            return total + rows * rows

        total = lax.fori_loop(0, ref.shape[0] // 8, body, jnp.zeros((8, ref.shape[1]), F32))
        return sum(total[:, at : at + 128] for at in range(0, ref.shape[1], 128))

    last = lax.axis_size("depth") - 1
    me = lax.axis_index("depth")
    zero = jnp.zeros(out.shape, F32)
    a = jnp.where(me != last, tile(mine), zero)
    out[...] = a + jnp.where(me != last - 1, tile(theirs), zero)


def times_chunk(e, matrix, body, low=None):
    rows = e.shape[0]
    e_high, e_low = halves(e)
    both = jnp.concatenate([e_high, e_low], 0)

    def part(cols):
        wide = dot(both, matrix[:, cols])
        product = wide[:rows] + wide[rows:]
        body(cols, product if low is None else product + dot(e_high, low[:, cols]))

    tiles(matrix.shape[1], HOP_TILE, part, True)


def hop_kernel(hop, received, *refs):
    source, c_high, c_low, sent, kept = refs[-5:]

    @pl.when(on_chip(hop + 1))
    def _():
        kept[...] = received[...]

        def body(cols, product):
            sent[:, cols] = received[:, cols] + source[:, cols] + product

        times_chunk(received[...], c_high, body, c_low)

    @pl.when(jnp.logical_not(on_chip(hop + 1)))
    def _():
        kept[...] = jnp.zeros_like(kept) if hop == 0 else refs[0][...]


def last_kernel(chunk, hop, received, before, r0_half, own_high, other_high, mine, sent):
    rows = received.shape[0]

    def body(kept, first, second, high):
        first[...] = kept

        def part(cols, product):
            second[:, cols] = (
                first[:, cols] + product + r0_half[chunk * rows : (chunk + 1) * rows, cols]
            )

        times_chunk(kept, high, part)

    e = jnp.where(on_chip(hop + 1), received[...], before[...])
    pl.when(on_core(0))(lambda: body(e, mine, sent, own_high))
    pl.when(on_core(1))(lambda: body(e, sent, mine, other_high))


def finish_kernel(count, *refs):
    mine, theirs = refs[:CHUNKS], refs[CHUNKS : 2 * CHUNKS]
    own_high, w, c, total, q0, k0, v0, o0, out, rms = refs[2 * CHUNKS : 2 * CHUNKS + 10]
    x, u, result, normed, context, sems = refs[2 * CHUNKS + 10 :]
    rows = mine[0].shape[0]
    half = rows * CHUNKS

    def gather(low, high):
        for j in range(CHUNKS):
            x[j * rows : (j + 1) * rows, :] = low[j][...]
            x[half + j * rows : half + (j + 1) * rows, :] = high[j][...]

    pl.when(on_core(0))(lambda: gather(mine, theirs))
    pl.when(on_core(1))(lambda: gather(theirs, mine))
    u[...] = c[...] + x[...]

    def carry(cols, product):
        result[1, :, cols] = w[:, cols] + x[:, cols] + product

    times_chunk(x[...], own_high, carry)
    mean_sq = jnp.sum(total[...], keepdims=True) / count
    rms[0] = jnp.sqrt(mean_sq)[0, 0]
    second = pltpu.make_async_copy(result.at[1], out.at[1], sems.at[0])
    second.start()
    layer(u, q0, k0, v0, o0, [lambda: None] * 4, normed, context, result.at[0])
    first = pltpu.make_async_copy(result.at[0], out.at[0], sems.at[1])
    first.start()
    first.wait()
    second.wait()


def per_device(c_states, w_query, w_key, w_value, w_out):
    dev_count = lax.axis_size("depth")
    chips = dev_count // 2
    tokens, width = c_states.shape[1:]
    half = tokens // 2
    rows = half // CHUNKS
    swap_pairs = [(i, i ^ 1) for i in range(dev_count)]
    dma = pltpu.SemaphoreType.DMA

    def swap(block):
        return lax.ppermute(block, "depth", swap_pairs)

    def f32_of(*shape):
        return pltpu.VMEM(shape, F32)

    def bf_of(*shape):
        return pltpu.VMEM(shape, BF)

    square = bf_of(width, width)
    state = f32_of(tokens, width)
    chunk = f32_of(rows, width)
    thin = bf_of(tokens, width)

    guess = c_states[0]
    c_states, w_query, w_key, w_value, w_out = (
        pltpu.with_memory_space_constraint(w, pltpu.HBM) for w in (c_states, w_query, w_key, w_value, w_out)
    )
    next_state = lax.ppermute(guess, "depth", [(i, i - 1) for i in range(1, dev_count)])
    own, own_high, query, key, value, c_guess = call(
        maps_kernel,
        (f32_of(width, width),) + (square,) * 4 + (state,),
        [IN_PLACE] * 5,
        1 << 20,
        limit=16,
        scratch=[square, square, dma((6,))],
    )(w_query, w_key, w_value, w_out, c_states)
    other = swap(own)
    query, key, value, c_guess = in_vmem(query, key, value, c_guess)
    fine_c, out_map = call(
        advance_kernel,
        (state, square),
        [IN_VMEM] * 4 + [IN_PLACE] * 4,
        1 << 20,
        limit=28,
        scratch=[square] * 4 + [state, thin, thin, dma((5,))],
    )(c_guess, query, key, value, w_query, w_key, w_value, w_out)
    fine_c, next_state = in_vmem(fine_c, next_state)
    residual = call(subtract_kernel, state, [IN_VMEM] * 2, 1 << 35, limit=4)(fine_c, next_state)
    other_residual = swap(residual)
    own, other, own_high = in_vmem(own, other, own_high)
    other_high, residual = in_vmem(
        call(cast_kernel, square, [IN_VMEM], 1 << 20, limit=4)(other), residual
    )
    c_high, c_low = call(
        functools.partial(product_kernel, False), (square, square), [IN_VMEM] * 4, 2 * width**3, limit=16
    )(own, other, own_high, other_high)
    other_residual, c_high = lax.optimization_barrier((other_residual, c_high))
    other_residual, c_high, c_low = in_vmem(other_residual, c_high, c_low)
    r0_half, *source = call(
        source_kernel,
        (f32_of(half, width),) + (chunk,) * CHUNKS,
        [IN_VMEM] * 4,
        4 * half * width * width,
    )(residual, other_residual, own_high, other_high)
    c_high, c_low = in_vmem(
        *call(
            functools.partial(product_kernel, True),
            (square, square),
            [IN_VMEM] * 6,
            2 * width**3,
            limit=16,
            aliases={4: 0, 5: 1},
        )(own, other, own_high, other_high, c_high, c_low)
    )
    sent = list(source)
    source = in_vmem(*source)
    kept = [None] * CHUNKS
    for hop in range(chips - 1):
        if hop == 3:
            residual, sent[-1] = lax.optimization_barrier((residual, sent[-1]))
            (residual,) = in_vmem(residual)
            total = call(squares_kernel, f32_of(8, 128), [IN_VMEM] * 2, 1 << 20, limit=4)(
                residual, other_residual
            )
        if hop in ROUNDS:
            reach = ROUNDS[hop]
            total, sent[-1] = lax.optimization_barrier((total, sent[-1]))
            theirs = lax.ppermute(total, "depth", [(i, i ^ reach) for i in range(dev_count)])
            total = call(add_kernel, f32_of(8, 128), [IN_VMEM] * 2, 1 << 12, limit=4)(total, theirs)
            kept[0], total = lax.optimization_barrier((kept[0], total))
        alike = [at for at in range(chips - 1) if group_of(at) == group_of(hop)]
        pairs = [(2 * at + i, 2 * at + 2 + i) for at in alike for i in range(2)]
        for j in range(CHUNKS):
            received = lax.ppermute(sent[j], "depth", pairs)
            held = in_vmem(received) if hop == 0 else in_vmem(received, kept[j])
            if hop < chips - 2:
                sent[j], kept[j] = call(
                    functools.partial(hop_kernel, hop),
                    (chunk, chunk),
                    [IN_VMEM] * (len(held) + 3),
                    4 * rows * width * width,
                    limit=4,
                )(*held, source[j], c_high, c_low)
            else:
                kept[j], sent[j] = call(
                    functools.partial(last_kernel, j, hop),
                    (chunk, chunk),
                    [IN_VMEM] * 5,
                    4 * rows * width * width,
                    limit=4,
                )(*held, r0_half, own_high, other_high)
    crossed = in_vmem(*[swap(block) for block in sent])
    kept = in_vmem(*kept)
    (out_map,) = in_vmem(out_map)
    return call(
        functools.partial(finish_kernel, float((dev_count - 1) * tokens * width)),
        (jax.ShapeDtypeStruct((2, tokens, width), F32), jax.ShapeDtypeStruct((1,), F32)),
        [IN_VMEM] * (2 * CHUNKS + 8),
        18 * tokens * width * width,
        limit=20,
        scratch=[state, state, f32_of(2, tokens, width), thin, thin, dma((2,))],
        out_specs=(IN_PLACE, IN_SMEM),
    )(*kept, *crossed, own_high, fine_c, c_guess, total, query, key, value, out_map)


def solution(mesh):
    in_specs = (
        P("depth", "dp", None),
        P("depth", None, None),
        P("depth", None, None),
        P("depth", None, None),
        P("depth", None, None),
    )
    out_specs = (P("depth", "dp", None), P("dp"))
    return jax.shard_map(
        per_device, mesh=mesh, in_specs=in_specs, out_specs=out_specs, check_vma=False
    )
```
